512 devices in a mesh: segment: 16 (over y, core), expert: 32 (over x, z).
Axes of the slice: x: 4, y: 8, z: 8, core: 2. Of those that a mesh axis runs over, the one named last changes fastest.
Arguments:
- state: bfloat16 [16, 256, 2048], P('segment', 'expert'), may hold values from -24 to 24
- routes: int32 [4, 16, 256, 2], P(None, 'segment', 'expert'), may hold values from 0 to 3, all different within a row; in each aligned block of 8 rows (0 to 7, 8 to 15, ..., all dimensions but the last counted through in order) at most 6 rows name the same one
- gates: float32 [4, 16, 256, 2], P(None, 'segment', 'expert'), may hold values from 0.2 to 1
- norm_gain: float32 [2, 16, 2048], P(None, 'segment'), may hold values from 0.25 to 1.75
- w_gate: bfloat16 [2, 16, 5120, 2048], P(None, 'segment', 'expert'), may hold values from -0.125 to 0.125
- w_up: bfloat16 [2, 16, 5120, 2048], P(None, 'segment', 'expert'), may hold values from -0.125 to 0.125
- w_down: bfloat16 [2, 16, 5120, 2048], P(None, 'segment', 'expert'), may hold values from -0.15625 to 0.15625
- spare_gate: bfloat16 [2, 16, 1280, 2048], P(None, 'segment', 'expert'), may hold values from -0.125 to 0.125
- spare_up: bfloat16 [2, 16, 1280, 2048], P(None, 'segment', 'expert'), may hold values from -0.125 to 0.125
- spare_down: bfloat16 [2, 16, 1280, 2048], P(None, 'segment', 'expert'), may hold values from -0.15625 to 0.15625
Outputs:
- final: bfloat16 [16, 256, 2048], P('segment', 'expert')
The draws below stay inside these ranges and needn't reach their ends.
Inputs may be any that keep to these rules, and one draw needn't show every extreme that they name: `routes`: each row names 2 different experts. Within the 8 rows of one device at one tick (aligned blocks), no expert is named by more than 6 rows, and some blocks reach 6.
All inputs are finite; a program needn't handle non-finite values.
Results may differ from the reference program's by a relative error of at most 0.012.
Values may be sent and summed in bfloat16 or wider, within the bound.
A program may use at most 64 MiB of HBM per device.

```python
import math
import jax
import jax.numpy as jnp
import numpy as np
from jax import lax

D = 2048
FE = 1280
EXPERTS = 4
TOPK = 2
TICKS = 4
TOK_DEV = 8
MOST = 6
CAP = 4
SEGMENTS = 16
TOKENS = 256
N_SEGMENT = 16
N_EXPERT = 32


def draw_state(key, part):
    base_key, column_key, row_key = jax.random.split(jax.random.fold_in(key, 11), 3)
    shape = (N_SEGMENT, TOKENS, D)
    base = jax.random.normal(base_key, shape, jnp.float32)
    columns = jnp.exp(jax.random.uniform(column_key, (D,), jnp.float32, math.log(0.3), math.log(3.0)))
    rows = jnp.exp(jax.random.uniform(row_key, (N_SEGMENT, TOKENS, 1), jnp.float32, math.log(0.5), math.log(2.0)))
    values = base * columns * rows
    return jnp.clip(values, -24.0, 24.0).astype(jnp.bfloat16)


def block_levels(rng, extent, cuts, smallest, high):
    factor_of = 1.0
    for dim, shards_of in cuts:
        steps = jax.random.uniform(jax.random.fold_in(jax.random.fold_in(rng, 6), dim), (shards_of,), jnp.float32, smallest / len(cuts), high / len(cuts))
        factor_of = factor_of * jnp.repeat(jnp.exp(steps), extent[dim] // shards_of).reshape((-1,) + (1,) * (len(extent) - 1 - dim))
    return factor_of


def deal_out(own_key, own, number, rows, number_of, top, limit, skew):
    ranking = jax.random.permutation(own_key, number_of)
    crowded, ordinary = portions_of(number_of, rows * top, limit, skew, True), portions_of(number_of, rows * top, limit, skew, False)
    places = jnp.arange(number_of)

    def named(tallies, rotation):
        used = int((tallies > 0).sum())
        fixed = max(1, used // 4)
        passed = fixed + (places - fixed + rotation * (used - fixed)) % max(1, number_of - fixed)
        return jnp.zeros((number_of,), jnp.int32).at[ranking[jnp.where(places < fixed, places, passed)]].set(jnp.asarray(tallies, jnp.int32))

    tallies = jnp.where(number % 4 == 0, named(crowded, number // 4), named(ordinary, number - number // 4 - 1))
    mixed = jax.random.permutation(jax.random.fold_in(own, 3), number_of)
    donor, sink = mixed[0:number_of // 2 * 2:2], mixed[1:number_of // 2 * 2:2]
    slack = jnp.minimum(tallies[donor] - 1, limit - tallies[sink]) // 2
    slack = jnp.where((donor == ranking[0]) | (sink == ranking[0]) | (tallies[sink] == 0), 0, jnp.maximum(slack, 0))
    passed = jax.random.randint(jax.random.fold_in(own, 4), (number_of // 2,), 0, 1 << 20) % (slack + 1)
    tallies = tallies.at[donor].add(-passed).at[sink].add(passed)
    items = jnp.searchsorted(jnp.cumsum(tallies), jnp.arange(rows * top), side="right").astype(jnp.int32)
    table = items.reshape(top, rows).T
    table = table[jax.random.permutation(jax.random.fold_in(own, 1), rows)]
    rotation = jax.random.randint(jax.random.fold_in(own, 2), (rows, 1), 0, top)
    return jnp.take_along_axis(table, (jnp.arange(top)[None, :] + rotation) % top, axis=1)


def portions_of(amount, total, reach, lean, full):
    loads = [(1 << 20) // math.isqrt(standing ** lean) + 1 for standing in range(1, amount + 1)]
    largest = reach if full else min(reach, max(-(-total // amount), total * loads[0] // sum(loads)))
    least = 1 if total - largest >= amount - 1 else 0
    counts, spare = [largest] + [least] * (amount - 1), total - largest - least * (amount - 1)
    while spare > 0:
        free = [i for i in range(1, amount) if counts[i] < largest] or [i for i in range(1, amount) if counts[i] < reach]
        whole, remaining = sum([loads[i] for i in free]), spare
        for i in free:
            extra = min(reach - counts[i], max(1, remaining * loads[i] // whole), spare)
            counts[i] = counts[i] + extra
            spare = spare - extra
    return np.array(counts)


def centred(key, extent, width, most, cuts=(), kind=jnp.bfloat16):
    values = jax.random.normal(key, extent, jnp.float32) * width
    if len(cuts) > 0:
        values = block_levels(key, extent, cuts, -0.22, 0.18) * values
    return jnp.clip(values, min=-most, max=most).astype(kind)


def setup_inputs(seed: int = 0) -> dict:
    key_of = jax.random.split(jax.random.key(seed), 11)
    state = draw_state(jax.random.fold_in(key_of[10], 71), 0)
    routes_keys = jax.random.split(jax.random.fold_in(key_of[1], 1), TICKS * SEGMENTS * TOKENS // TOK_DEV)
    routes_turns = jax.random.permutation(jax.random.fold_in(key_of[1], 3), TICKS * SEGMENTS * TOKENS // TOK_DEV)
    routes = jax.vmap(lambda own, number: deal_out(jax.random.fold_in(key_of[1], 2), own, number, TOK_DEV, EXPERTS, TOPK, MOST, 2))(routes_keys, routes_turns).reshape((TICKS, SEGMENTS, TOKENS, TOPK))
    gates = jnp.clip(jnp.exp(math.log(1.0) - 1.609438 * jax.random.uniform(key_of[2], (TICKS, SEGMENTS, TOKENS, TOPK), jnp.float32) ** block_levels(key_of[2], (TICKS, SEGMENTS, TOKENS, TOPK), ((1, 16), (2, 32)), -0.2, 0.2)), 0.2, 1.0)
    norm_gain = jnp.clip(1.0 + 0.15 * jax.random.normal(key_of[3], (2, SEGMENTS, D), jnp.float32), 0.25, 1.75)
    w_gate = centred(key_of[4], (2, SEGMENTS, EXPERTS * FE, D), D ** -0.5, 0.125, ((1, 16), (2, 32)))
    w_up = centred(key_of[5], (2, SEGMENTS, EXPERTS * FE, D), D ** -0.5, 0.125, ((1, 16), (2, 32)))
    w_down = centred(key_of[6], (2, SEGMENTS, EXPERTS * FE, D), FE ** -0.5, 0.15625, ((1, 16), (2, 32)))
    spare_gate = centred(key_of[7], (2, SEGMENTS, FE, D), D ** -0.5, 0.125, ((1, 16), (2, 32)))
    spare_up = centred(key_of[8], (2, SEGMENTS, FE, D), D ** -0.5, 0.125, ((1, 16), (2, 32)))
    spare_down = centred(key_of[9], (2, SEGMENTS, FE, D), FE ** -0.5, 0.15625, ((1, 16), (2, 32)))
    return dict(state=state, routes=routes, gates=gates, norm_gain=norm_gain, w_gate=w_gate, w_up=w_up, w_down=w_down, spare_gate=spare_gate, spare_up=spare_up, spare_down=spare_down)


EPSILON = 1e-06

def rms_normed(rows, norm_scale):
    values = rows.astype(jnp.float32)
    row_scale = lax.rsqrt(lax.optimization_barrier(jnp.mean(values * values, axis=-1, keepdims=True)) + EPSILON)
    return (values * row_scale * norm_scale).astype(jnp.bfloat16)

def expert_output(normed, gate_rows, up_rows, down_rows, split_count):
    row_count = normed.shape[0]
    hidden_part = gate_rows.shape[0] // split_count
    gate_pre = jnp.dot(normed, gate_rows.astype(jnp.float32).T, precision=lax.Precision.HIGHEST)
    up_pre = jnp.dot(normed, up_rows.astype(jnp.float32).T, precision=lax.Precision.HIGHEST)
    hidden = lax.optimization_barrier((jax.nn.silu(gate_pre) * up_pre).astype(jnp.bfloat16)).astype(jnp.float32)
    pieces = hidden.reshape(row_count, split_count, hidden_part)
    down_pieces = down_rows.astype(jnp.float32).reshape(split_count, hidden_part, D)
    partial_value = jnp.einsum('tph,phd->tpd', pieces, down_pieces, precision=lax.Precision.HIGHEST)
    partial_value = lax.optimization_barrier(partial_value.astype(jnp.bfloat16)).astype(jnp.float32)
    return lax.optimization_barrier(jnp.sum(partial_value, axis=1))

def moe_layer(current, chosen, weights, norm_scale, gate_all, up_all, down_all, spare_g, spare_u, spare_d):
    normed = rms_normed(current, norm_scale).astype(jnp.float32)
    split_count = N_EXPERT // EXPERTS
    labels = jnp.arange(EXPERTS, dtype=jnp.int32)
    member = jnp.any(chosen[:, :, None] == labels[None, None, :], axis=1)
    taken = member.astype(jnp.int32).reshape(-1, TOK_DEV, EXPERTS)
    position = (jnp.cumsum(taken, axis=1, dtype=jnp.int32) - taken).reshape(-1, EXPERTS)
    combined = jnp.zeros(current.shape, jnp.float32)
    spill = jnp.zeros((current.shape[0],), jnp.float32)
    for expert_idx in range(EXPERTS):
        low = expert_idx * FE
        output = expert_output(normed, gate_all[low:low + FE], up_all[low:low + FE], down_all[low:low + FE], split_count)
        whole = lax.optimization_barrier(jnp.sum(jnp.where(chosen == expert_idx, weights, jnp.float32(0.0)), axis=1))
        inside = position[:, expert_idx] < CAP
        share = jnp.where(inside, whole, jnp.float32(0.0))
        spill = spill + jnp.where(inside, jnp.float32(0.0), whole)
        combined = combined + share[:, None] * output
    spare_out = expert_output(normed, spare_g, spare_u, spare_d, N_EXPERT)
    combined = combined + spill[:, None] * spare_out
    return (current.astype(jnp.float32) + combined).astype(jnp.bfloat16)

def select_layer(table, group_idx, segment_idx):
    inner = lax.dynamic_index_in_dim(table, group_idx, 0, keepdims=False)
    return lax.dynamic_index_in_dim(inner, segment_idx, 0, keepdims=False)

def reference(state, routes, gates, norm_gain, w_gate, w_up, w_down, spare_gate, spare_up, spare_down):
    current = state
    for tick_idx in range(TICKS):

        def one_segment(segment_idx):
            start_segment = (segment_idx - tick_idx) % N_SEGMENT
            first_group = jnp.where((start_segment % 2 == 1) & (start_segment + TICKS <= N_SEGMENT), 1, 0)
            group_idx = (first_group + jnp.where(start_segment + tick_idx >= N_SEGMENT, 1, 0)).astype(jnp.int32)
            holder = ((segment_idx + 1) % N_SEGMENT).astype(jnp.int32)
            return moe_layer(current[segment_idx], routes[tick_idx, segment_idx], gates[tick_idx, segment_idx], select_layer(norm_gain, group_idx, segment_idx), select_layer(w_gate, group_idx, segment_idx), select_layer(w_up, group_idx, segment_idx), select_layer(w_down, group_idx, segment_idx), select_layer(spare_gate, group_idx, holder), select_layer(spare_up, group_idx, holder), select_layer(spare_down, group_idx, holder))
        updated = lax.map(one_segment, jnp.arange(N_SEGMENT, dtype=jnp.int32))
        if tick_idx + 1 < TICKS:
            current = jnp.roll(updated, 1, axis=0)
        else:
            current = updated
    return current
```

```python
import functools

import jax
import jax.numpy as jnp
from jax import lax
from jax.experimental import pallas as pl
from jax.experimental.pallas import tpu as pltpu
from jax.sharding import PartitionSpec as P

EXPERTS = 4
TICKS = 4
CAP = 4
EPSILON = 1e-06
LANES = 128
MESH = pl.DeviceIdType.MESH
F32 = jnp.float32
BF16 = jnp.bfloat16

BZ_NEAR, BZ_FAR, BX_WHOLE, BX_HALF, AX, AZ = 0, 4, 7, 9, 11, 14
RBX_HALF, RBX_WHOLE, RAZ, RBZ, RAX = 22, 24, 26, 34, 41
COPIES = 44


def group_of(section, tick_idx, segments):
    start = lax.rem(section - tick_idx + segments, segments)
    odd = lax.rem(start, 2) == 1
    first = jnp.where(odd & (start + TICKS <= segments), 1, 0)
    return first + jnp.where(start + tick_idx >= segments, 1, 0)


def kernel(
    segments, nx, nz,
    state, routes, gates, gain, w_gate, w_up, w_down, spare_g, spare_u, spare_d,
    out,
    cur, nxt, coef, gw, uw, dw, xa, xb, pa, pb, ra1, ra, qf, qa, rqa, rb1, rb2, sb, rz,
    send_sem, recv_sem, shift_send, shift_recv, w_sem, spare_send, spare_recv,
):
    tok, width = state.shape
    aw = pa.shape[-1]
    bw = pb.shape[-1]
    rows = nx * nz * tok
    home, extra = w_gate.shape[1], spare_g.shape[1]
    slices = gw.shape[1]
    s = lax.axis_index("segment")
    mine = lax.axis_index("expert")
    x, z = mine // nz, lax.rem(mine, nz)
    half_z, half_x = nz // 2, nx // 2
    odd = lax.rem(z, 2)
    turn = 1 - 2 * odd

    def xo(k):
        return lax.rem(x + k + nx, nx)

    def zo(k):
        return lax.rem(z + k + nz, nz)

    def at(xx, zz):
        return (s, xx * nz + zz)

    after = (lax.rem(s + 1, segments), mine)
    before = (lax.rem(s + segments - 1, segments), mine)

    loads = []
    for i, (source, store) in enumerate(((w_gate, gw), (w_up, uw), (w_down, dw))):
        load = pltpu.make_async_copy(source, store.at[:, pl.ds(0, home)], w_sem.at[i])
        load.start()
        loads.append(load)

    barrier = pltpu.get_barrier_semaphore()
    peers = [at(xo(1), z), at(xo(2), z), at(xo(3), z)]
    peers += [at(x, zo(1)), at(x, zo(-1)), at(x, zo(2)), at(x, zo(-2)), after, before]
    for peer in peers:
        pl.semaphore_signal(barrier, inc=1, device_id=peer, device_id_type=MESH)

    for store in (gw, uw, dw):
        store[:, home + extra :] = jnp.zeros((2, slices - home - extra, tok, width), BF16)
    cur[0] = state[...]

    lane = lax.broadcasted_iota(jnp.int32, (tok, LANES), 1)
    row = lax.broadcasted_iota(jnp.int32, (tok, LANES), 0)
    label, low, of_tick = lane % 8, (lane // 8) % 2, lane // 16
    packed = jnp.zeros((tok, LANES), F32)
    for t in range(TICKS):
        chosen, weights = routes[t], gates[t]
        hit0, hit1 = chosen[:, 0:1] == label, chosen[:, 1:2] == label
        member = jnp.where(hit0 | hit1, 1.0, 0.0)
        whole = jnp.where(hit0, weights[:, 0:1], 0.0) + jnp.where(hit1, weights[:, 1:2], 0.0)
        position = jnp.zeros((tok, LANES), F32)
        for i in range(tok - 1):
            position = position + jnp.where(row > i, member[i : i + 1], 0.0)
        inside = position < CAP
        over = jnp.where(inside | (lane >= EXPERTS), 0.0, whole)
        spill = jnp.sum(over, axis=1, keepdims=True)
        value = jnp.where(label == EXPERTS, spill, jnp.where(inside, whole, 0.0))
        top = value.astype(BF16).astype(F32)
        packed = jnp.where(of_tick == t, jnp.where(low == 1, value - top, top), packed)
    coef[...] = packed.astype(BF16)

    pl.semaphore_wait(barrier, len(peers))

    first_there = group_of(before[0], 0, segments)
    first_here = group_of(s, 0, segments)
    spares = []
    for order in range(2):
        there = first_there if order == 0 else 1 - first_there
        for i, (source, store) in enumerate(((spare_g, gw), (spare_u, uw), (spare_d, dw))):
            copy = pltpu.make_async_remote_copy(
                source.at[there],
                store.at[there, pl.ds(home, extra)],
                spare_send.at[order, i],
                spare_recv.at[order, i],
                device_id=before,
                device_id_type=MESH,
            )
            copy.start()
            spares.append(copy)

    def spare_wait(order):
        here = first_here if order == 0 else 1 - first_here
        for i, (source, store) in enumerate(((spare_g, gw), (spare_u, uw), (spare_d, dw))):
            pltpu.make_async_remote_copy(
                source.at[here],
                store.at[here, pl.ds(home, extra)],
                spare_send.at[order, i],
                spare_recv.at[order, i],
                device_id=before,
                device_id_type=MESH,
            ).wait_recv()

    def shift_copy(t):
        return pltpu.make_async_remote_copy(
            nxt.at[t],
            cur.at[t + 1],
            shift_send.at[t],
            shift_recv.at[t],
            device_id=after,
            device_id_type=MESH,
        )

    def tick(t, carry):
        group = group_of(s, t, segments)
        started = []

        def send(number, source, target, peer):
            copy = pltpu.make_async_remote_copy(
                source,
                target,
                send_sem.at[t, number],
                recv_sem.at[t, number],
                device_id=peer,
                device_id_type=MESH,
            )
            copy.start()
            started.append(copy)

        def arrived(number, landing):
            pltpu.make_async_remote_copy(
                landing,
                landing,
                send_sem.at[t, number],
                recv_sem.at[t, number],
                device_id=after,
                device_id_type=MESH,
            ).wait_recv()

        @pl.when(t > 0)
        def _():
            shift_copy(t - 1).wait_recv()

        values = cur[t].astype(F32)
        scale = lax.rsqrt(jnp.mean(values * values, axis=-1, keepdims=True) + EPSILON)
        normed = (values * scale * gain[group]).astype(BF16)
        xa[t, z, x, :, :aw] = normed[:, :aw]
        xa[t, z, x, :, aw:] = coef[...]
        xb[t, z, x] = normed[:, aw:]

        for off in (1, 2, 3):
            send(AX + off - 1, xa.at[t, z, x], xa.at[t, z, x], at(xo(off), z))
        for i, off in enumerate((1, -1, 2, -2)):
            send(BZ_NEAR + i, xb.at[t, z, x], xb.at[t, z, x], at(x, zo(off)))

        def a_step(k):
            if k == 4:
                right, left = pl.ds(0, half_x), pl.ds(half_x, half_x)
            else:
                right = left = pl.ds(0, nx)
            block = xa.at[t, zo(1 - k), right]
            send(AZ + 2 * k - 2, block, block, at(x, zo(1)))
            block = xa.at[t, zo(k - 1), left]
            send(AZ + 2 * k - 1, block, block, at(x, zo(-1)))

        def a_arrived(k):
            if k == 4:
                right, left = pl.ds(0, half_x), pl.ds(half_x, half_x)
            else:
                right = left = pl.ds(0, nx)
            arrived(AZ + 2 * k - 2, xa.at[t, zo(-k), right])
            arrived(AZ + 2 * k - 1, xa.at[t, zo(k), left])

        for i, off in enumerate((1, -1, 2, -2)):
            arrived(BZ_NEAR + i, xb.at[t, zo(-off), x])
        block = xb.at[t, zo(-2), x]
        send(BZ_FAR, block, block, at(x, zo(1)))
        block = xb.at[t, zo(2), x]
        send(BZ_FAR + 1, block, block, at(x, zo(-1)))
        block = xb.at[t, zo(-2 * turn), x]
        send(BZ_FAR + 2, block, block, at(x, zo(2 * turn)))
        for off in (1, 2, 3):
            arrived(AX + off - 1, xa.at[t, z, xo(-off)])
        a_step(1)
        arrived(BZ_FAR, xb.at[t, zo(-3), x])
        arrived(BZ_FAR + 1, xb.at[t, zo(3), x])
        arrived(BZ_FAR + 2, xb.at[t, zo(4), x])
        block = xb.at[t, :, x]
        send(BX_WHOLE, block, block, at(xo(1), z))
        send(BX_WHOLE + 1, block, block, at(xo(-1), z))
        a_arrived(1)
        a_step(2)
        a_arrived(2)
        a_step(3)
        arrived(BX_WHOLE, xb.at[t, :, xo(-1)])
        block = xb.at[t, pl.ds(0, half_z), xo(-1)]
        send(BX_HALF, block, block, at(xo(1), z))
        arrived(BX_WHOLE + 1, xb.at[t, :, xo(1)])
        block = xb.at[t, pl.ds(half_z, half_z), xo(1)]
        send(BX_HALF + 1, block, block, at(xo(-1), z))
        a_arrived(3)
        a_step(4)

        @pl.when(t == 0)
        def _():
            for load in loads:
                load.wait()
            spare_wait(0)

        @pl.when(t == 1)
        def _():
            spare_wait(1)

        arrived(BX_HALF, xb.at[t, pl.ds(0, half_z), xo(2)])
        arrived(BX_HALF + 1, xb.at[t, pl.ds(half_z, half_z), xo(2)])
        a_arrived(4)

        a_rows = xa.at[t].reshape(rows, aw + LANES)
        b_rows = xb.at[t].reshape(rows, bw)
        gate_w = gw.at[group].reshape(slices * tok, width)
        up_w = uw.at[group].reshape(slices * tok, width)
        down_w = dw.at[group].reshape(slices * tok, width)
        contract = (((1,), (1,)), ((), ()))

        def product(weight):
            return lax.dot_general(
                a_rows[:, :aw], weight[:, :aw], contract, preferred_element_type=F32
            ) + lax.dot_general(b_rows[...], weight[:, aw:], contract, preferred_element_type=F32)

        gate = product(gate_w)
        up = product(up_w)
        factors = a_rows[:, aw:].astype(F32)
        lanes = lax.broadcasted_iota(jnp.int32, factors.shape, 1)
        base = t * 16

        def factor(which):
            spot = (lanes == base + which) | (lanes == base + which + 8)
            return jnp.sum(jnp.where(spot, factors, 0.0), axis=1, keepdims=True)

        units = lax.broadcasted_iota(jnp.int32, gate.shape, 1)
        scales = jnp.where(units < home * tok, factor(x), factor(EXPERTS))
        hidden = (gate / (1.0 + jnp.exp(-gate)) * up * scales).astype(BF16)
        pb.reshape(rows, bw)[...] = jnp.dot(
            hidden, down_w[:, aw:], preferred_element_type=F32
        ).astype(BF16)

        send(RBX_HALF, pb.at[pl.ds(0, half_z), xo(2)], rb1.at[t, 0], at(xo(1), z))
        send(RBX_HALF + 1, pb.at[pl.ds(half_z, half_z), xo(2)], rb1.at[t, 1], at(xo(-1), z))
        pa.reshape(rows, aw)[...] = jnp.dot(
            hidden, down_w[:, :aw], preferred_element_type=F32
        ).astype(BF16)
        send(RAZ, pa.at[zo(4), pl.ds(0, half_x)], ra1.at[t, 0], at(x, zo(1)))
        send(RAZ + 1, pa.at[zo(4), pl.ds(half_x, half_x)], ra1.at[t, 1], at(x, zo(-1)))

        def plus(first, *more):
            total = first.astype(F32)
            for term in more:
                total = total + term.astype(F32)
            return total

        def add_first(side):
            cut = pl.ds(side * half_x, half_x)
            to = zo(3 - 6 * side)
            arrived(RAZ + side, ra1.at[t, side])
            pa[to, cut] = plus(pa[to, cut], ra1[t, side]).astype(BF16)
            send(RAZ + 2 + side, pa.at[to], ra.at[t, 0, side], at(x, zo(1 - 2 * side)))

        def add_next(side, k):
            to = zo((4 - k) * (1 - 2 * side))
            arrived(RAZ + 2 * k - 2 + side, ra.at[t, k - 2, side])
            pa[to] = plus(pa[to], ra[t, k - 2, side]).astype(BF16)
            send(RAZ + 2 * k + side, pa.at[to], ra.at[t, k - 1, side], at(x, zo(1 - 2 * side)))

        def add_b(side):
            cut = pl.ds(side * half_z, half_z)
            to = xo(1 - 2 * side)
            arrived(RBX_HALF + side, rb1.at[t, side])
            pb[cut, to] = plus(pb[cut, to], rb1[t, side]).astype(BF16)
            send(RBX_WHOLE + side, pb.at[:, to], rb2.at[t, side], at(to, z))

        add_b(0)
        add_b(1)
        add_first(0)
        add_first(1)
        for k in (2, 3):
            add_next(0, k)
            add_next(1, k)
        arrived(RBX_WHOLE, rb2.at[t, 0])
        arrived(RBX_WHOLE + 1, rb2.at[t, 1])
        sb[...] = plus(pb[:, x], rb2[t, 0], rb2[t, 1]).astype(BF16)
        send(RBZ + 4, sb.at[zo(4)], rz.at[t, 4], at(x, zo(2 * turn)))
        send(RBZ + 2, sb.at[zo(3)], rz.at[t, 2], at(x, zo(1)))
        send(RBZ + 3, sb.at[zo(-3)], rz.at[t, 3], at(x, zo(-1)))
        send(RBZ, sb.at[zo(1)], rz.at[t, 0], at(x, zo(1)))
        send(RBZ + 1, sb.at[zo(-1)], rz.at[t, 1], at(x, zo(-1)))
        arrived(RAZ + 6, ra.at[t, 2, 0])
        arrived(RAZ + 7, ra.at[t, 2, 1])
        total = plus(pa[z], ra[t, 2, 0], ra[t, 2, 1])
        qf[...] = total
        qa[...] = total.astype(BF16)
        for off in (1, 2, 3):
            send(RAX + off - 1, qa.at[xo(off)], rqa.at[t, off - 1], at(xo(off), z))
        for i in (2, 3, 4):
            arrived(RBZ + i, rz.at[t, i])
        far, near = zo(2 * turn), zo(-2 * turn)
        sb[far] = plus(sb[far], rz[t, 2 + odd], rz[t, 4]).astype(BF16)
        sb[near] = plus(sb[near], rz[t, 3 - odd]).astype(BF16)
        send(RBZ + 5, sb.at[zo(2)], rz.at[t, 5], at(x, zo(2)))
        send(RBZ + 6, sb.at[zo(-2)], rz.at[t, 6], at(x, zo(-2)))
        for i in (0, 1):
            arrived(RBZ + i, rz.at[t, i])
        part_b = plus(pb[z, x], rb2[t, 0, z], rb2[t, 1, z], rz[t, 0], rz[t, 1])
        for off in (1, 2, 3):
            arrived(RAX + off - 1, rqa.at[t, off - 1])
        part_a = plus(qf[x], rqa[t, 0], rqa[t, 1], rqa[t, 2])
        nxt[t, :, :aw] = (cur[t, :, :aw].astype(F32) + part_a).astype(BF16)
        for i in (5, 6):
            arrived(RBZ + i, rz.at[t, i])
        part_b = plus(part_b, rz[t, 5], rz[t, 6])
        nxt[t, :, aw:] = (cur[t, :, aw:].astype(F32) + part_b).astype(BF16)

        @pl.when(t + 1 < TICKS)
        def _():
            shift_copy(t).start()

        for copy in started:
            copy.wait_send()
        return carry

    lax.fori_loop(0, TICKS, tick, 0)
    out[...] = nxt[TICKS - 1]
    for t in range(TICKS - 1):
        shift_copy(t).wait_send()
    for copy in spares:
        copy.wait_send()


def on_device(
    state, routes, gates, norm_gain, w_gate, w_up, w_down, spare_gate, spare_up, spare_down
):
    segments = lax.axis_size("segment")
    members = lax.axis_size("expert")
    nx = EXPERTS
    nz = members // nx
    tok, width = state.shape[1:]
    aw = max(1, width // LANES * 7 // 16) * LANES
    bw = width - aw
    home, extra = w_gate.shape[2], spare_gate.shape[2]
    units = -(-(home + extra) // 256) * 256

    def cut(weights):
        return weights.reshape(2, weights.shape[2] // tok, tok, width)

    vmem, anywhere = pl.BlockSpec(memory_space=pltpu.VMEM), pl.BlockSpec(memory_space=pl.ANY)
    store = pltpu.VMEM((2, units // tok, tok, width), BF16)
    final = pl.pallas_call(
        functools.partial(kernel, segments, nx, nz),
        out_shape=jax.ShapeDtypeStruct((tok, width), BF16),
        in_specs=[vmem] * 4 + [anywhere] * 6,
        out_specs=vmem,
        scratch_shapes=[
            pltpu.VMEM((TICKS, tok, width), BF16),
            pltpu.VMEM((TICKS, tok, width), BF16),
            pltpu.VMEM((tok, LANES), BF16),
            store,
            store,
            store,
            pltpu.VMEM((TICKS, nz, nx, tok, aw + LANES), BF16),
            pltpu.VMEM((TICKS, nz, nx, tok, bw), BF16),
            pltpu.VMEM((nz, nx, tok, aw), BF16),
            pltpu.VMEM((nz, nx, tok, bw), BF16),
            pltpu.VMEM((TICKS, 2, nx // 2, tok, aw), BF16),
            pltpu.VMEM((TICKS, 3, 2, nx, tok, aw), BF16),
            pltpu.VMEM((nx, tok, aw), F32),
            pltpu.VMEM((nx, tok, aw), BF16),
            pltpu.VMEM((TICKS, 3, tok, aw), BF16),
            pltpu.VMEM((TICKS, 2, nz // 2, tok, bw), BF16),
            pltpu.VMEM((TICKS, 2, nz, tok, bw), BF16),
            pltpu.VMEM((nz, tok, bw), BF16),
            pltpu.VMEM((TICKS, 7, tok, bw), BF16),
            pltpu.SemaphoreType.DMA((TICKS, COPIES)),
            pltpu.SemaphoreType.DMA((TICKS, COPIES)),
            pltpu.SemaphoreType.DMA((TICKS - 1,)),
            pltpu.SemaphoreType.DMA((TICKS - 1,)),
            pltpu.SemaphoreType.DMA((3,)),
            pltpu.SemaphoreType.DMA((2, 3)),
            pltpu.SemaphoreType.DMA((2, 3)),
        ],
        compiler_params=pltpu.CompilerParams(
            collective_id=0, has_side_effects=True, vmem_limit_bytes=44 * 1024 * 1024
        ),
    )(
        state[0],
        routes[:, 0],
        gates[:, 0],
        norm_gain,
        cut(w_gate),
        cut(w_up),
        cut(w_down),
        cut(spare_gate),
        cut(spare_up),
        cut(spare_down),
    )
    return final[None]


def solution(mesh):
    return jax.shard_map(
        on_device,
        mesh=mesh,
        in_specs=(
            P("segment", "expert", None),
            P(None, "segment", "expert", None),
            P(None, "segment", "expert", None),
            P(None, "segment", None),
            P(None, "segment", "expert", None),
            P(None, "segment", "expert", None),
            P(None, "segment", "expert", None),
            P(None, "segment", "expert", None),
            P(None, "segment", "expert", None),
            P(None, "segment", "expert", None),
        ),
        out_specs=P("segment", "expert", None),
        check_vma=False,
    )
```

```python
import functools
import math

import jax
import jax.numpy as jnp
from jax import lax
from jax.experimental import pallas as pl
from jax.experimental.pallas import tpu as pltpu
from jax.sharding import PartitionSpec as P

EXPERTS = 4
TICKS = 4
CAP = 4
EPSILON = 1e-06
LANES = 128
MESH = pl.DeviceIdType.MESH
F32 = jnp.float32
BF16 = jnp.bfloat16

def group_of(section, tick_idx, segments):
    start = lax.rem(section - tick_idx + segments, segments)
    odd = lax.rem(start, 2) == 1
    first = jnp.where(odd & (start + TICKS <= segments), 1, 0)
    return first + jnp.where(start + tick_idx >= segments, 1, 0)


ORDER = (0, 1, -1, 2, -2, 3, -3, 4)
NZ, NX = 8, 4
GZ, GX, SX, SZ = 0, 8, 32, 56
COPIES = 64


def slot_from(offset):
    return next(i for i, d in enumerate(ORDER) if (d + offset) % NZ == 0)


def flat(ref):
    return ref.reshape(math.prod(ref.shape[:-1]), ref.shape[-1])


def put(ref, value):
    flat(ref)[...] = value


def kernel(
    segments,
    state, routes, gates, gain, w_gate, w_up, w_down, spare_g, spare_u, spare_d,
    out,
    cur, routes_v, gates_v, gain_v, coef, gw, uw, dw, xb, hid, pb, rx, sb, res, parts,
    send_sem, recv_sem, res_send, res_recv, w_sem, spare_send, spare_recv, coef_send, coef_recv,
):
    tok, width = state.shape
    home, extra = w_gate.shape[1], spare_g.shape[1]
    units = gw.shape[1] * tok
    half = NZ // 2
    rows = half * NX * tok
    s = lax.axis_index("segment")
    mine = lax.axis_index("expert")
    x, z = mine // NZ, lax.rem(mine, NZ)
    s_after = lax.rem(s + 1, segments)
    s_before = lax.rem(s + segments - 1, segments)

    def at(section, off_x, off_z):
        return (section, lax.rem(x + off_x + NX, NX) * NZ + lax.rem(z + off_z + NZ, NZ))

    before, after = (s_before, mine), (s_after, mine)

    loads = []
    for i, (source, store) in enumerate(
        (
            (state, cur.at[0]),
            (routes, routes_v),
            (gates, gates_v),
            (gain, gain_v),
            (w_gate, gw.at[:, pl.ds(0, home)]),
            (w_up, uw.at[:, pl.ds(0, home)]),
            (w_down, dw.at[:, pl.ds(0, home)]),
        )
    ):
        load = pltpu.make_async_copy(source, store, w_sem.at[i])
        load.start()
        loads.append(load)

    barrier = pltpu.get_barrier_semaphore()
    peers = [at(s, off, 0) for off in range(1, NX)]
    peers += [at(s, 0, off) for off in range(1, NZ)]
    for section in (s_after, s_before):
        peers += [at(section, 0, off) for off in range(NZ)]
    for peer in peers:
        pl.semaphore_signal(barrier, inc=1, device_id=peer, device_id_type=MESH)

    for store in (gw, uw, dw):
        unused = gw.shape[1] - home - extra
        store[:, home + extra :] = jnp.zeros((2, unused, tok, width), BF16)

    lane = lax.broadcasted_iota(jnp.int32, (tok, LANES), 1)
    row = lax.broadcasted_iota(jnp.int32, (tok, LANES), 0)
    diagonal = row[:, :tok] == lane[:, :tok]
    label = (lane % 8).astype(F32)
    low, of_tick = (lane // 8) % 2, lane // 16

    def upright(line):
        line = jnp.broadcast_to(line, (tok, tok))
        return jnp.sum(jnp.where(diagonal, line, 0.0), axis=1, keepdims=True)

    for load in loads[:4]:
        load.wait()
    packed = jnp.zeros((tok, LANES), F32)
    for t in range(TICKS):
        chosen, weights = routes_v[t].astype(F32), gates_v[t]
        hit0, hit1 = upright(chosen[0:1]) == label, upright(chosen[1:2]) == label
        member = jnp.where(hit0 | hit1, 1.0, 0.0)
        whole = jnp.where(hit0, upright(weights[0:1]), 0.0)
        whole = whole + jnp.where(hit1, upright(weights[1:2]), 0.0)
        position = jnp.zeros((tok, LANES), F32)
        for i in range(tok - 1):
            position = position + jnp.where(row > i, member[i : i + 1], 0.0)
        inside = position < CAP
        over = jnp.where(inside | (lane >= EXPERTS), 0.0, whole)
        spill = jnp.sum(over, axis=1, keepdims=True)
        value = jnp.where(label == EXPERTS, spill, jnp.where(inside, whole, 0.0))
        top = value.astype(BF16).astype(F32)
        packed = jnp.where(of_tick == t, jnp.where(low == 1, value - top, top), packed)
    coef[0, 0] = packed.astype(BF16)

    pl.semaphore_wait(barrier, len(peers))

    def remote(source, target, sent, got, peer):
        return pltpu.make_async_remote_copy(
            source, target, sent, got, device_id=peer, device_id_type=MESH
        )

    first_there = group_of(s_before, 0, segments)
    first_here = group_of(s, 0, segments)
    spare_pairs = ((spare_g, gw), (spare_u, uw), (spare_d, dw))

    def spare_copy(order, i, first):
        source, store = spare_pairs[i]
        part = first if order == 0 else 1 - first
        return remote(
            source.at[part],
            store.at[part, pl.ds(home, extra)],
            spare_send.at[order, i],
            spare_recv.at[order, i],
            before,
        )

    def coef_z(j, peer):
        return remote(coef.at[0, 0], coef.at[j, 0], coef_send.at[j], coef_recv.at[j], peer)

    def coef_x(o, peer):
        n = NZ - 1 + o
        return remote(coef.at[:, 0], coef.at[:, o], coef_send.at[n], coef_recv.at[n], peer)

    def res_copy(t):
        return remote(cur.at[t], res.at[t], res_send.at[t], res_recv.at[t], after)

    def back_copy(t, i, peer):
        j = slot_from(ORDER[i])
        n = SZ + j
        return remote(sb.at[t, i], parts.at[t, j], send_sem.at[t, n], recv_sem.at[t, n], peer)

    def landed(t):
        for j in range(NZ - 1, -1, -1):
            target = parts.at[t, j]
            n = SZ + j
            if j == 0:
                @pl.when(t < TICKS - 1)
                def _():
                    remote(target, target, send_sem.at[t, n], recv_sem.at[t, n], after).wait_recv()
            else:
                remote(target, target, send_sem.at[t, n], recv_sem.at[t, n], after).wait_recv()
        total = parts[t, NZ - 1].astype(F32)
        for j in range(NZ - 2, -1, -1):
            total = total + parts[t, j].astype(F32)
        return total

    def tick(t, carry):
        group = group_of(s, t, segments)
        started = []

        def send(number, source, target, peer):
            copy = remote(source, target, send_sem.at[t, number], recv_sem.at[t, number], peer)
            copy.start()
            started.append(copy)

        def arrived(number, landing):
            remote(
                landing, landing, send_sem.at[t, number], recv_sem.at[t, number], after
            ).wait_recv()

        @pl.when(t > 0)
        def _():
            res_copy(t - 1).wait_recv()
            cur[t] = (res[t - 1].astype(F32) + landed(t - 1)).astype(BF16)

        values = cur[t].astype(F32)
        scale = lax.rsqrt(jnp.mean(values * values, axis=-1, keepdims=True) + EPSILON)
        xb[t, 0, 0] = (values * scale * gain_v[group]).astype(BF16)

        def gather_z(i):
            j = slot_from(ORDER[i])
            send(GZ + j, xb.at[t, 0, 0], xb.at[t, j, 0], at(s, 0, ORDER[i]))

        def gather_x(i):
            for off in range(1, NX):
                o = NX - off
                send(GX + i * 3 + o - 1, xb.at[t, i, 0], xb.at[t, i, o], at(s, off, 0))

        def gathered_x(i):
            for o in range(1, NX):
                arrived(GX + i * 3 + o - 1, xb.at[t, i, o])

        gather_z(1)
        gather_z(2)
        gather_x(0)
        for i in range(3, NZ):
            gather_z(i)

        @pl.when(t == 0)
        def _():
            for order in range(2):
                for i in range(3):
                    spare_copy(order, i, first_there).start()
            for i in range(1, NZ):
                coef_z(slot_from(ORDER[i]), at(s, 0, ORDER[i])).start()

        @pl.when(t < TICKS - 1)
        def _():
            res_copy(t).start()

        for i in range(1, NZ):
            arrived(GZ + i, xb.at[t, i, 0])
            gather_x(i)

        @pl.when(t == 0)
        def _():
            for j in range(1, NZ):
                coef_z(j, after).wait_recv()
            for off in range(1, NX):
                coef_x(NX - off, at(s, off, 0)).start()
            for load in loads[4:]:
                load.wait()
            for i in range(3):
                spare_copy(0, i, first_here).wait_recv()
            for o in range(1, NX):
                coef_x(o, after).wait_recv()

        @pl.when(t == 1)
        def _():
            for i in range(3):
                spare_copy(1, i, first_here).wait_recv()

        gate_w, up_w, down_w = flat(gw.at[group]), flat(uw.at[group]), flat(dw.at[group])
        contract = (((1,), (1,)), ((), ()))
        lanes = lax.broadcasted_iota(jnp.int32, (rows, LANES), 1)
        unit = lax.broadcasted_iota(jnp.int32, (rows, units), 1)
        base = t * 16

        for c in range(2):
            blocks = pl.ds(c * half, half)
            for i in range(c * half, c * half + half):
                gathered_x(i)
            normed = flat(xb.at[t, blocks])[...]
            gate = lax.dot_general(normed, gate_w[...], contract, preferred_element_type=F32)
            up = lax.dot_general(normed, up_w[...], contract, preferred_element_type=F32)
            factors = flat(coef.at[blocks])[...].astype(F32)

            def factor(which):
                spot = (lanes == base + which) | (lanes == base + which + 8)
                return jnp.sum(jnp.where(spot, factors, 0.0), axis=1, keepdims=True)

            scales = jnp.where(unit < home * tok, factor(x), factor(EXPERTS))
            hidden = gate / (1.0 + jnp.exp(-gate)) * up * scales
            hid[pl.ds(c * rows, rows)] = hidden.astype(BF16)

        for c in (1, 0):
            put(
                pb.at[pl.ds(c * half, half)],
                jnp.dot(
                    hid[pl.ds(c * rows, rows)], down_w[...], preferred_element_type=F32
                ).astype(BF16),
            )
            for i in range(c * half + half - 1, c * half - 1, -1):
                for off in range(1, NX):
                    o = NX - off
                    send(SX + i * 3 + o - 1, pb.at[i, off], rx.at[t, i, o - 1], at(s, off, 0))

        last = t == TICKS - 1
        to = jnp.where(last, s, s_after)
        for i in range(NZ - 1, -1, -1):
            for o in range(1, NX):
                arrived(SX + i * 3 + o - 1, rx.at[t, i, o - 1])
            total = pb[i, 0].astype(F32)
            for o in range(1, NX):
                total = total + rx[t, i, o - 1].astype(F32)
            sb[t, i] = total.astype(BF16)
            if i > 0:
                back_copy(t, i, at(to, 0, ORDER[i])).start()

        @pl.when(t < TICKS - 1)
        def _():
            back_copy(t, 0, after).start()

        @pl.when(last)
        def _():
            parts[t, 0] = sb[t, 0]

        for copy in started:
            copy.wait_send()

        return carry

    lax.fori_loop(0, TICKS, tick, 0)
    out[...] = (cur[TICKS - 1].astype(F32) + landed(TICKS - 1)).astype(BF16)
    for t in range(TICKS):
        for i in range(1, NZ):
            back_copy(t, i, after).wait_send()
        if t < TICKS - 1:
            back_copy(t, 0, after).wait_send()
            res_copy(t).wait_send()
    for i in range(3):
        for order in range(2):
            spare_copy(order, i, first_there).wait_send()
    for i in range(1, NZ):
        coef_z(i, after).wait_send()
    for o in range(1, NX):
        coef_x(o, after).wait_send()


def on_device(
    state, routes, gates, norm_gain, w_gate, w_up, w_down, spare_gate, spare_up, spare_down
):
    tok, width = state.shape[1:]
    home, extra = w_gate.shape[2], spare_gate.shape[2]
    units = -(-(home + extra) // 256) * 256

    def cut(weights):
        return weights.reshape(2, weights.shape[2] // tok, tok, width)

    vmem, hbm = pl.BlockSpec(memory_space=pltpu.VMEM), pl.BlockSpec(memory_space=pltpu.HBM)
    store = pltpu.VMEM((2, units // tok, tok, width), BF16)
    dma = pltpu.SemaphoreType.DMA
    final = pl.pallas_call(
        functools.partial(kernel, lax.axis_size("segment")),
        out_shape=jax.ShapeDtypeStruct((tok, width), BF16),
        in_specs=[hbm] * 10,
        out_specs=vmem,
        scratch_shapes=[
            pltpu.VMEM((TICKS, tok, width), BF16),
            pltpu.VMEM((TICKS, 2, tok), jnp.int32),
            pltpu.VMEM((TICKS, 2, tok), F32),
            pltpu.VMEM((2, 1, width), F32),
            pltpu.VMEM((NZ, NX, tok, LANES), BF16),
            store,
            store,
            store,
            pltpu.VMEM((TICKS, NZ, NX, tok, width), BF16),
            pltpu.VMEM((NZ * NX * tok, units), BF16),
            pltpu.VMEM((NZ, NX, tok, width), BF16),
            pltpu.VMEM((TICKS, NZ, NX - 1, tok, width), BF16),
            pltpu.VMEM((TICKS, NZ, tok, width), BF16),
            pltpu.VMEM((TICKS - 1, tok, width), BF16),
            pltpu.VMEM((TICKS, NZ, tok, width), BF16),
            dma((TICKS, COPIES)),
            dma((TICKS, COPIES)),
            dma((TICKS - 1,)),
            dma((TICKS - 1,)),
            dma((7,)),
            dma((2, 3)),
            dma((2, 3)),
            dma((NZ + NX - 1,)),
            dma((NZ + NX - 1,)),
        ],
        compiler_params=pltpu.CompilerParams(
            collective_id=0, has_side_effects=True, vmem_limit_bytes=60 * 1024 * 1024
        ),
    )(
        state[0],
        jnp.swapaxes(routes[:, 0], 1, 2),
        jnp.swapaxes(gates[:, 0], 1, 2),
        norm_gain,
        cut(w_gate),
        cut(w_up),
        cut(w_down),
        cut(spare_gate),
        cut(spare_up),
        cut(spare_down),
    )
    return final[None]


def solution(mesh):
    return jax.shard_map(
        on_device,
        mesh=mesh,
        in_specs=(
            P("segment", "expert", None),
            P(None, "segment", "expert", None),
            P(None, "segment", "expert", None),
            P(None, "segment", None),
            P(None, "segment", "expert", None),
            P(None, "segment", "expert", None),
            P(None, "segment", "expert", None),
            P(None, "segment", "expert", None),
            P(None, "segment", "expert", None),
            P(None, "segment", "expert", None),
        ),
        out_specs=P("segment", "expert", None),
        check_vma=False,
    )
```

```python
import functools
import math

import jax
import jax.numpy as jnp
from jax import lax
from jax.experimental import pallas as pl
from jax.experimental.pallas import tpu as pltpu
from jax.sharding import PartitionSpec as P

EXPERTS = 4
TICKS = 4
CAP = 4
EPSILON = 1e-06
LANES = 128
MESH = pl.DeviceIdType.MESH
F32 = jnp.float32
BF16 = jnp.bfloat16

def group_of(section, tick_idx, segments):
    start = lax.rem(section - tick_idx + segments, segments)
    odd = lax.rem(start, 2) == 1
    first = jnp.where(odd & (start + TICKS <= segments), 1, 0)
    return first + jnp.where(start + tick_idx >= segments, 1, 0)


ORDER = (0, 4, 3, -3, 2, -2, 1, -1)
NZ, NX = 8, 4
X_FIRST = 512
X_LAST = 512
GX, SX, GZ, GAX, GAZ, SAZ = 0, 8, 16, 24, 25, 27
GROUPS = 28
SENT_GZ, SENT_GX, SENT_GAX, SENT_GAZ, SENT_SX, SENT_SAZ = range(6)
BACK = (1, 2, 3, 0, 4, 5, 6, 7)
A_AFTER = 5


def slot_from(offset):
    return next(i for i, d in enumerate(ORDER) if (d + offset) % NZ == 0)


def flat(ref):
    return ref.reshape(math.prod(ref.shape[:-1]), ref.shape[-1])


def put(ref, value):
    flat(ref)[...] = value


def kernel(
    segments,
    state, routes, gates, gain, w_gate, w_up, w_down, spare_g, spare_u, spare_d,
    out,
    cur, routes_v, gates_v, gain_v, coef, gw, uw, dw, xa, xb, hid, pa, pb, ra, rx, sa, sb, res,
    parts_a, parts_b,
    send_sem, recv_sem, back_send, back_recv, res_send, res_recv, w_sem, spare_send, spare_recv, coef_send, coef_recv,
):
    tok, width = state.shape
    home, extra = w_gate.shape[1], spare_g.shape[1]
    units = gw.shape[1] * tok
    aw, lw = xa.shape[-1], pa.shape[-1]
    half = NZ // 2
    rows = half * NX * tok
    s = lax.axis_index("segment")
    mine = lax.axis_index("expert")
    x, z = mine // NZ, lax.rem(mine, NZ)
    s_after = lax.rem(s + 1, segments)
    s_before = lax.rem(s + segments - 1, segments)

    def at(section, off_x, off_z):
        return (section, lax.rem(x + off_x + NX, NX) * NZ + lax.rem(z + off_z + NZ, NZ))

    before, after = (s_before, mine), (s_after, mine)

    loads = []
    for i, (source, store) in enumerate(
        (
            (state, cur.at[0]),
            (routes, routes_v),
            (gates, gates_v),
            (gain, gain_v),
            (w_gate, gw.at[:, pl.ds(0, home)]),
            (w_up, uw.at[:, pl.ds(0, home)]),
            (w_down, dw.at[:, pl.ds(0, home)]),
        )
    ):
        load = pltpu.make_async_copy(source, store, w_sem.at[i])
        load.start()
        loads.append(load)

    barrier = pltpu.get_barrier_semaphore()
    peers = [at(s, off, 0) for off in range(1, NX)]
    peers += [at(s, 0, off) for off in range(1, NZ)]
    for section in (s_after, s_before):
        peers += [at(section, 0, off) for off in range(NZ)]
        peers += [at(section, off, 0) for off in range(1, NX)]
    for peer in peers:
        pl.semaphore_signal(barrier, inc=1, device_id=peer, device_id_type=MESH)

    for store in (gw, uw, dw):
        unused = gw.shape[1] - home - extra
        store[:, home + extra :] = jnp.zeros((2, unused, tok, width), BF16)

    lane = lax.broadcasted_iota(jnp.int32, (tok, LANES), 1)
    row = lax.broadcasted_iota(jnp.int32, (tok, LANES), 0)
    diagonal = row[:, :tok] == lane[:, :tok]
    label = (lane % 8).astype(F32)
    low, of_tick = (lane // 8) % 2, lane // 16

    def upright(line):
        line = jnp.broadcast_to(line, (tok, tok))
        return jnp.sum(jnp.where(diagonal, line, 0.0), axis=1, keepdims=True)

    for load in loads[:4]:
        load.wait()
    packed = jnp.zeros((tok, LANES), F32)
    for t in range(TICKS):
        chosen, weights = routes_v[t].astype(F32), gates_v[t]
        hit0, hit1 = upright(chosen[0:1]) == label, upright(chosen[1:2]) == label
        member = jnp.where(hit0 | hit1, 1.0, 0.0)
        whole = jnp.where(hit0, upright(weights[0:1]), 0.0)
        whole = whole + jnp.where(hit1, upright(weights[1:2]), 0.0)
        position = jnp.zeros((tok, LANES), F32)
        for i in range(tok - 1):
            position = position + jnp.where(row > i, member[i : i + 1], 0.0)
        inside = position < CAP
        over = jnp.where(inside | (lane >= EXPERTS), 0.0, whole)
        spill = jnp.sum(over, axis=1, keepdims=True)
        value = jnp.where(label == EXPERTS, spill, jnp.where(inside, whole, 0.0))
        top = value.astype(BF16).astype(F32)
        packed = jnp.where(of_tick == t, jnp.where(low == 1, value - top, top), packed)
    coef[0, 0] = packed.astype(BF16)

    pl.semaphore_wait(barrier, len(peers))

    def remote(source, target, sent, got, peer):
        return pltpu.make_async_remote_copy(
            source, target, sent, got, device_id=peer, device_id_type=MESH
        )

    first_there = group_of(s_before, 0, segments)
    first_here = group_of(s, 0, segments)
    spare_pairs = ((spare_g, gw), (spare_u, uw), (spare_d, dw))

    def spare_copy(order, i, first):
        source, store = spare_pairs[i]
        part = first if order == 0 else 1 - first
        return remote(
            source.at[part],
            store.at[part, pl.ds(home, extra)],
            spare_send.at[order, i],
            spare_recv.at[order, i],
            before,
        )

    def coef_z(j, peer):
        return remote(coef.at[0, 0], coef.at[j, 0], coef_send.at[0], coef_recv.at[0], peer)

    def coef_x(o, peer):
        return remote(coef.at[:, 0], coef.at[:, o], coef_send.at[1], coef_recv.at[1], peer)

    def group(ref, sent, got):
        return remote(ref, ref, sent, got, after)

    coefs_z = group(coef.at[pl.ds(1, NZ - 1), 0], coef_send.at[0], coef_recv.at[0])
    coefs_x = group(coef.at[:, pl.ds(1, NX - 1)], coef_send.at[1], coef_recv.at[1])

    def res_copy(t):
        return remote(cur.at[t], res.at[t], res_send.at[t], res_recv.at[t], after)

    def back_sem(t, i, first):
        n = first if i > 0 else first + 2
        return back_send.at[t, n], back_recv.at[t, n]

    def back_b(t, i, peer):
        return remote(sb.at[t, i], parts_b.at[t, slot_from(ORDER[i])], *back_sem(t, i, 0), peer)

    def back_a(t, off, peer):
        o = (NX - off) % NX
        return remote(sa.at[t, off], parts_a.at[t, o], *back_sem(t, off, 1), peer)

    def back_groups(t):
        return (
            group(parts_b.at[t, pl.ds(1, NZ - 1)], *back_sem(t, 1, 0)),
            group(parts_a.at[t, pl.ds(1, NX - 1)], *back_sem(t, 1, 1)),
        )

    def back_own(t):
        return back_b(t, 0, after), back_a(t, 0, after)

    def landed(t):
        for copies in back_groups(t):
            copies.wait_recv()

        @pl.when(t < TICKS - 1)
        def _():
            for copy in back_own(t):
                copy.wait_recv()

        sums = []
        for parts, count in ((parts_a, NX), (parts_b, NZ)):
            total = parts[t, 0].astype(F32)
            for j in range(1, count):
                total = total + parts[t, j].astype(F32)
            sums.append(total)
        return sums

    def next_state(base, t):
        sum_a, sum_b = landed(t)
        base = base.astype(F32)
        return (base[:, :lw] + sum_a).astype(BF16), (base[:, lw:] + sum_b).astype(BF16)

    def tick(t, carry):
        layer = group_of(s, t, segments)

        def send(sent, got, source, target, peer):
            remote(source, target, send_sem.at[sent], recv_sem.at[got], peer).start()

        def arrived(got, landing):
            group(landing, send_sem.at[0], recv_sem.at[got]).wait_recv()

        def left(sent, shape_of):
            group(shape_of, send_sem.at[sent], recv_sem.at[0]).wait_send()

        @pl.when(t > 0)
        def _():
            res_copy(t - 1).wait_recv()
            cur[t, :, :lw], cur[t, :, lw:] = next_state(res[t - 1], t - 1)

        values = cur[t].astype(F32)
        scale = lax.rsqrt(jnp.mean(values * values, axis=-1, keepdims=True) + EPSILON)
        normed = (values * scale * gain_v[layer]).astype(BF16)
        xa[t, 0, 0] = normed[:, :aw]
        xb[t, 0, 0] = normed[:, aw:]

        def gather_z(i):
            j = slot_from(ORDER[i])
            send(SENT_GZ, GZ + j, xb.at[t, 0, 0], xb.at[t, j, 0], at(s, 0, ORDER[i]))

        def gather_x(i):
            for off in range(1, NX):
                o = NX - off
                send(SENT_GX, GX + i, xb.at[t, i, 0], xb.at[t, i, o], at(s, off, 0))

        def gathered_x(i):
            arrived(GX + i, xb.at[t, i, pl.ds(1, NX - 1)])

        for off in range(1, NX):
            o = NX - off
            send(SENT_GAX, GAX, xa.at[t, 0, 0], xa.at[t, 0, o], at(s, off, 0))
        gather_z(1)
        gather_z(2)
        gather_x(0)
        for i in range(3, NZ):
            gather_z(i)

        @pl.when(t == 0)
        def _():
            for order in range(2):
                for i in range(3):
                    spare_copy(order, i, first_there).start()
            for i in range(1, NZ):
                coef_z(slot_from(ORDER[i]), at(s, 0, ORDER[i])).start()

        @pl.when(t < TICKS - 1)
        def _():
            res_copy(t).start()

        for i in range(1, NZ):
            arrived(GZ + i, xb.at[t, i, 0])
            gather_x(i)
            if i == 2:
                arrived(GAX, xa.at[t, 0, pl.ds(1, NX - 1)])
                for k in range(1, NZ):
                    j = slot_from(ORDER[k])
                    send(SENT_GAZ, GAZ + j // half, xa.at[t, 0], xa.at[t, j], at(s, 0, ORDER[k]))

        @pl.when(t == 0)
        def _():
            coefs_z.wait_recv()
            for off in range(1, NX):
                coef_x(NX - off, at(s, off, 0)).start()
            for load in loads[4:]:
                load.wait()
            for i in range(3):
                spare_copy(0, i, first_here).wait_recv()
            coefs_x.wait_recv()

        @pl.when(t == 1)
        def _():
            for i in range(3):
                spare_copy(1, i, first_here).wait_recv()

        gate_w, up_w, down_w = flat(gw.at[layer]), flat(uw.at[layer]), flat(dw.at[layer])
        contract = (((1,), (1,)), ((), ()))
        lanes = lax.broadcasted_iota(jnp.int32, (rows, LANES), 1)
        unit = lax.broadcasted_iota(jnp.int32, (rows, units), 1)
        base = t * 16

        for c in range(2):
            blocks = pl.ds(c * half, half)
            for i in range(c * half, c * half + half):
                gathered_x(i)
            arrived(GAZ + c, xa.at[t, pl.ds(c * half + 1 - c, half - 1 + c)])
            rows_a, rows_b = flat(xa.at[t, blocks])[...], flat(xb.at[t, blocks])[...]

            def product(weight):
                return lax.dot_general(
                    rows_a, weight[:, :aw], contract, preferred_element_type=F32
                ) + lax.dot_general(
                    rows_b, weight[:, aw:], contract, preferred_element_type=F32
                )

            gate, up = product(gate_w), product(up_w)
            factors = flat(coef.at[blocks])[...].astype(F32)

            def factor(which):
                spot = (lanes == base + which) | (lanes == base + which + 8)
                return jnp.sum(jnp.where(spot, factors, 0.0), axis=1, keepdims=True)

            scales = jnp.where(unit < home * tok, factor(x), factor(EXPERTS))
            hidden = gate / (1.0 + jnp.exp(-gate)) * up * scales
            hid[pl.ds(c * rows, rows)] = hidden.astype(BF16)


            for part, columns in ((pb, slice(lw, width)), (pa, slice(0, lw))):
                put(
                    part.at[blocks],
                    jnp.dot(
                        hid[pl.ds(c * rows, rows)],
                        down_w[:, columns],
                        preferred_element_type=F32,
                    ).astype(BF16),
                )
            for i in range(c * half, c * half + half):
                for off in range(1, NX):
                    o = NX - off
                    send(SENT_SX, SX + i, pb.at[i, off], rx.at[t, i, o - 1], at(s, off, 0))
                if i > 0:
                    j = slot_from(ORDER[i])
                    send(SENT_SAZ, SAZ, pa.at[i], ra.at[t, j], at(s, 0, ORDER[i]))

        last = t == TICKS - 1
        to = jnp.where(last, s, s_after)
        for i in BACK:
            arrived(SX + i, rx.at[t, i])
            total = pb[i, 0].astype(F32)
            for o in range(1, NX):
                total = total + rx[t, i, o - 1].astype(F32)
            sb[t, i] = total.astype(BF16)
            if i > 0:
                back_b(t, i, at(to, 0, ORDER[i])).start()
            if i == A_AFTER:
                arrived(SAZ, ra.at[t, pl.ds(1, NZ - 1)])
                total = pa[0].astype(F32)
                for j in range(1, NZ):
                    total = total + ra[t, j].astype(F32)
                sa[t] = total.astype(BF16)
                for off in range(1, NX):
                    back_a(t, off, at(to, off, 0)).start()

        @pl.when(t < TICKS - 1)
        def _():
            for copy in back_own(t):
                copy.start()

        @pl.when(last)
        def _():
            parts_b[t, 0] = sb[t, 0]
            parts_a[t, 0] = sa[t, 0]

        left(SENT_GZ, xb.at[t, pl.ds(1, NZ - 1), 0])
        left(SENT_GX, xb.at[t, :, pl.ds(1, NX - 1)])
        left(SENT_GAX, xa.at[t, 0, pl.ds(1, NX - 1)])
        left(SENT_GAZ, xa.at[t, pl.ds(1, NZ - 1)])
        left(SENT_SX, rx.at[t])
        left(SENT_SAZ, ra.at[t, pl.ds(1, NZ - 1)])

        return carry

    lax.fori_loop(0, TICKS, tick, 0)
    out[:, :lw], out[:, lw:] = next_state(cur[TICKS - 1], TICKS - 1)
    for t in range(TICKS):
        for copies in back_groups(t):
            copies.wait_send()
        if t < TICKS - 1:
            for copy in back_own(t):
                copy.wait_send()
            res_copy(t).wait_send()
    for i in range(3):
        for order in range(2):
            spare_copy(order, i, first_there).wait_send()
    coefs_z.wait_send()
    coefs_x.wait_send()


def on_device(
    state, routes, gates, norm_gain, w_gate, w_up, w_down, spare_gate, spare_up, spare_down
):
    tok, width = state.shape[1:]
    home, extra = w_gate.shape[2], spare_gate.shape[2]
    units = -(-(home + extra) // 256) * 256
    aw = min(X_FIRST, width // 2)
    bw = width - aw
    lw = min(X_LAST, width // 2)
    rw = width - lw

    def cut(weights):
        return weights.reshape(2, weights.shape[2] // tok, tok, width)

    vmem, hbm = pl.BlockSpec(memory_space=pltpu.VMEM), pl.BlockSpec(memory_space=pltpu.HBM)
    store = pltpu.VMEM((2, units // tok, tok, width), BF16)
    dma = pltpu.SemaphoreType.DMA
    final = pl.pallas_call(
        functools.partial(kernel, lax.axis_size("segment")),
        out_shape=jax.ShapeDtypeStruct((tok, width), BF16),
        in_specs=[hbm] * 10,
        out_specs=vmem,
        scratch_shapes=[
            pltpu.VMEM((TICKS, tok, width), BF16),
            pltpu.VMEM((TICKS, 2, tok), jnp.int32),
            pltpu.VMEM((TICKS, 2, tok), F32),
            pltpu.VMEM((2, 1, width), F32),
            pltpu.VMEM((NZ, NX, tok, LANES), BF16),
            store,
            store,
            store,
            pltpu.VMEM((TICKS, NZ, NX, tok, aw), BF16),
            pltpu.VMEM((TICKS, NZ, NX, tok, bw), BF16),
            pltpu.VMEM((NZ * NX * tok, units), BF16),
            pltpu.VMEM((NZ, NX, tok, lw), BF16),
            pltpu.VMEM((NZ, NX, tok, rw), BF16),
            pltpu.VMEM((TICKS, NZ, NX, tok, lw), BF16),
            pltpu.VMEM((TICKS, NZ, NX - 1, tok, rw), BF16),
            pltpu.VMEM((TICKS, NX, tok, lw), BF16),
            pltpu.VMEM((TICKS, NZ, tok, rw), BF16),
            pltpu.VMEM((TICKS - 1, tok, width), BF16),
            pltpu.VMEM((TICKS, NX, tok, lw), BF16),
            pltpu.VMEM((TICKS, NZ, tok, rw), BF16),
            dma((6,)),
            dma((GROUPS,)),
            dma((TICKS, 4)),
            dma((TICKS, 4)),
            dma((TICKS - 1,)),
            dma((TICKS - 1,)),
            dma((7,)),
            dma((2, 3)),
            dma((2, 3)),
            dma((2,)),
            dma((2,)),
        ],
        compiler_params=pltpu.CompilerParams(
            collective_id=0, has_side_effects=True, vmem_limit_bytes=60 * 1024 * 1024
        ),
    )(
        state[0],
        jnp.swapaxes(routes[:, 0], 1, 2),
        jnp.swapaxes(gates[:, 0], 1, 2),
        norm_gain,
        cut(w_gate),
        cut(w_up),
        cut(w_down),
        cut(spare_gate),
        cut(spare_up),
        cut(spare_down),
    )
    return final[None]


def solution(mesh):
    return jax.shard_map(
        on_device,
        mesh=mesh,
        in_specs=(
            P("segment", "expert", None),
            P(None, "segment", "expert", None),
            P(None, "segment", "expert", None),
            P(None, "segment", None),
            P(None, "segment", "expert", None),
            P(None, "segment", "expert", None),
            P(None, "segment", "expert", None),
            P(None, "segment", "expert", None),
            P(None, "segment", "expert", None),
            P(None, "segment", "expert", None),
        ),
        out_specs=P("segment", "expert", None),
        check_vma=False,
    )
```

```python
import functools
import math

import jax
import jax.numpy as jnp
from jax import lax
from jax.experimental import pallas as pl
from jax.experimental.pallas import tpu as pltpu
from jax.sharding import PartitionSpec as P

EXPERTS = 4
TICKS = 4
CAP = 4
EPSILON = 1e-06
LANES = 128
MESH = pl.DeviceIdType.MESH
F32 = jnp.float32
BF16 = jnp.bfloat16

def group_of(section, tick_idx, segments):
    start = lax.rem(section - tick_idx + segments, segments)
    odd = lax.rem(start, 2) == 1
    first = jnp.where(odd & (start + TICKS <= segments), 1, 0)
    return first + jnp.where(start + tick_idx >= segments, 1, 0)


ORDER = (0, 1, -1, 4, 3, -3, 2, -2)
NZ, NX = 8, 4
X_FIRST = 512
X_LAST = 512
GX, SX, GZ, GAX, SAZ, GAZ = 0, 8, 16, 24, 25, 26
CHUNKS = ((0, 3), (3, 6), (6, 8))
GROUPS = GAZ + len(CHUNKS)
SENT_GZ, SENT_GX, SENT_GAX, SENT_GAZ, SENT_SX, SENT_SAZ = range(6)
BACK = (1, 2, 0, 3, 4, 5, 6, 7)
A_AFTER = 5


def slot_from(offset):
    return next(i for i, d in enumerate(ORDER) if (d + offset) % NZ == 0)


def chunk_of(slot):
    return next(c for c, (low, high) in enumerate(CHUNKS) if low <= slot < high)


def flat(ref):
    return ref.reshape(math.prod(ref.shape[:-1]), ref.shape[-1])


def put(ref, value):
    flat(ref)[...] = value


def kernel(
    segments,
    state, routes, gates, gain, w_gate, w_up, w_down, spare_g, spare_u, spare_d,
    out,
    cur, routes_v, gates_v, gain_v, coef, gw, uw, dw, xa, xb, hid, pa, pb, ra, rx, sa, sb, res,
    parts_a, parts_b,
    send_sem, recv_sem, back_send, back_recv, res_send, res_recv, w_sem, spare_send, spare_recv, coef_send, coef_recv,
):
    tok, width = state.shape
    home, extra = w_gate.shape[1], spare_g.shape[1]
    units = gw.shape[1] * tok
    aw, lw = xa.shape[-1], pa.shape[-1]
    s = lax.axis_index("segment")
    mine = lax.axis_index("expert")
    x, z = mine // NZ, lax.rem(mine, NZ)
    s_after = lax.rem(s + 1, segments)
    s_before = lax.rem(s + segments - 1, segments)

    def at(section, off_x, off_z):
        return (section, lax.rem(x + off_x + NX, NX) * NZ + lax.rem(z + off_z + NZ, NZ))

    before, after = (s_before, mine), (s_after, mine)

    loads = []
    for i, (source, store) in enumerate(
        (
            (state, cur.at[0]),
            (routes, routes_v),
            (gates, gates_v),
            (gain, gain_v),
            (w_gate, gw.at[:, pl.ds(0, home)]),
            (w_up, uw.at[:, pl.ds(0, home)]),
            (w_down, dw.at[:, pl.ds(0, home)]),
        )
    ):
        load = pltpu.make_async_copy(source, store, w_sem.at[i])
        load.start()
        loads.append(load)

    barrier = pltpu.get_barrier_semaphore()
    peers = [at(s, off, 0) for off in range(1, NX)]
    peers += [at(s, 0, off) for off in range(1, NZ)]
    for section in (s_after, s_before):
        peers += [at(section, 0, off) for off in range(NZ)]
        peers += [at(section, off, 0) for off in range(1, NX)]
    for peer in peers:
        pl.semaphore_signal(barrier, inc=1, device_id=peer, device_id_type=MESH)

    for store in (gw, uw, dw):
        unused = gw.shape[1] - home - extra
        store[:, home + extra :] = jnp.zeros((2, unused, tok, width), BF16)

    lane = lax.broadcasted_iota(jnp.int32, (tok, LANES), 1)
    row = lax.broadcasted_iota(jnp.int32, (tok, LANES), 0)
    diagonal = row[:, :tok] == lane[:, :tok]
    label = (lane % 8).astype(F32)
    low, of_tick = (lane // 8) % 2, lane // 16

    def upright(line):
        line = jnp.broadcast_to(line, (tok, tok))
        return jnp.sum(jnp.where(diagonal, line, 0.0), axis=1, keepdims=True)

    for load in loads[:4]:
        load.wait()
    packed = jnp.zeros((tok, LANES), F32)
    for t in range(TICKS):
        chosen, weights = routes_v[t].astype(F32), gates_v[t]
        hit0, hit1 = upright(chosen[0:1]) == label, upright(chosen[1:2]) == label
        member = jnp.where(hit0 | hit1, 1.0, 0.0)
        whole = jnp.where(hit0, upright(weights[0:1]), 0.0)
        whole = whole + jnp.where(hit1, upright(weights[1:2]), 0.0)
        position = jnp.zeros((tok, LANES), F32)
        for i in range(tok - 1):
            position = position + jnp.where(row > i, member[i : i + 1], 0.0)
        inside = position < CAP
        over = jnp.where(inside | (lane >= EXPERTS), 0.0, whole)
        spill = jnp.sum(over, axis=1, keepdims=True)
        value = jnp.where(label == EXPERTS, spill, jnp.where(inside, whole, 0.0))
        top = value.astype(BF16).astype(F32)
        packed = jnp.where(of_tick == t, jnp.where(low == 1, value - top, top), packed)
    coef[0, 0] = packed.astype(BF16)

    pl.semaphore_wait(barrier, len(peers))

    def remote(source, target, sent, got, peer):
        return pltpu.make_async_remote_copy(
            source, target, sent, got, device_id=peer, device_id_type=MESH
        )

    first_there = group_of(s_before, 0, segments)
    first_here = group_of(s, 0, segments)
    spare_pairs = ((spare_g, gw), (spare_u, uw), (spare_d, dw))

    def spare_copy(order, i, first):
        source, store = spare_pairs[i]
        part = first if order == 0 else 1 - first
        return remote(
            source.at[part],
            store.at[part, pl.ds(home, extra)],
            spare_send.at[order, i],
            spare_recv.at[order, i],
            before,
        )

    def coef_z(j, peer):
        return remote(coef.at[0, 0], coef.at[j, 0], coef_send.at[0], coef_recv.at[0], peer)

    def coef_x(o, peer):
        return remote(coef.at[:, 0], coef.at[:, o], coef_send.at[1], coef_recv.at[1], peer)

    def group(ref, sent, got):
        return remote(ref, ref, sent, got, after)

    coefs_z = group(coef.at[pl.ds(1, NZ - 1), 0], coef_send.at[0], coef_recv.at[0])
    coefs_x = group(coef.at[:, pl.ds(1, NX - 1)], coef_send.at[1], coef_recv.at[1])

    def res_copy(t):
        return remote(cur.at[t], res.at[t], res_send.at[t], res_recv.at[t], after)

    def back_sem(t, i, first):
        n = first if i > 0 else first + 2
        return back_send.at[t, n], back_recv.at[t, n]

    def back_b(t, i, peer):
        return remote(sb.at[t, i], parts_b.at[t, slot_from(ORDER[i])], *back_sem(t, i, 0), peer)

    def back_a(t, off, peer):
        o = (NX - off) % NX
        return remote(sa.at[t, off], parts_a.at[t, o], *back_sem(t, off, 1), peer)

    def back_groups(t):
        return (
            group(parts_b.at[t, pl.ds(1, NZ - 1)], *back_sem(t, 1, 0)),
            group(parts_a.at[t, pl.ds(1, NX - 1)], *back_sem(t, 1, 1)),
        )

    def back_own(t):
        return back_b(t, 0, after), back_a(t, 0, after)

    def landed(t):
        for copies in back_groups(t):
            copies.wait_recv()

        @pl.when(t < TICKS - 1)
        def _():
            for copy in back_own(t):
                copy.wait_recv()

        sums = []
        for parts, count in ((parts_a, NX), (parts_b, NZ)):
            total = parts[t, 0].astype(F32)
            for j in range(1, count):
                total = total + parts[t, j].astype(F32)
            sums.append(total)
        return sums

    def next_state(base, t):
        sum_a, sum_b = landed(t)
        base = base.astype(F32)
        return (base[:, :lw] + sum_a).astype(BF16), (base[:, lw:] + sum_b).astype(BF16)

    def tick(t, carry):
        layer = group_of(s, t, segments)

        def send(sent, got, source, target, peer):
            remote(source, target, send_sem.at[sent], recv_sem.at[got], peer).start()

        def arrived(got, landing):
            group(landing, send_sem.at[0], recv_sem.at[got]).wait_recv()

        def left(sent, shape_of):
            group(shape_of, send_sem.at[sent], recv_sem.at[0]).wait_send()

        @pl.when(t > 0)
        def _():
            res_copy(t - 1).wait_recv()
            cur[t, :, :lw], cur[t, :, lw:] = next_state(res[t - 1], t - 1)

        values = cur[t].astype(F32)
        scale = lax.rsqrt(jnp.mean(values * values, axis=-1, keepdims=True) + EPSILON)
        normed = (values * scale * gain_v[layer]).astype(BF16)
        xa[t, 0, 0] = normed[:, :aw]
        xb[t, 0, 0] = normed[:, aw:]

        def gather_z(i):
            j = slot_from(ORDER[i])
            send(SENT_GZ, GZ + j, xb.at[t, 0, 0], xb.at[t, j, 0], at(s, 0, ORDER[i]))

        def gather_x(i):
            for off in range(1, NX):
                o = NX - off
                send(SENT_GX, GX + i, xb.at[t, i, 0], xb.at[t, i, o], at(s, off, 0))

        def gathered_x(i):
            arrived(GX + i, xb.at[t, i, pl.ds(1, NX - 1)])

        @pl.when(t == 0)
        def _():
            for i in range(1, NZ):
                coef_z(slot_from(ORDER[i]), at(s, 0, ORDER[i])).start()

        for off in range(1, NX):
            o = NX - off
            send(SENT_GAX, GAX, xa.at[t, 0, 0], xa.at[t, 0, o], at(s, off, 0))
        gather_z(1)
        gather_z(2)
        gather_x(0)
        for i in range(3, NZ):
            gather_z(i)

        @pl.when(t == 0)
        def _():
            for order in range(2):
                for i in range(3):
                    spare_copy(order, i, first_there).start()

        @pl.when(t < TICKS - 1)
        def _():
            res_copy(t).start()

        for i in range(1, NZ):
            arrived(GZ + i, xb.at[t, i, 0])
            gather_x(i)
            if i == 2:
                @pl.when(t == 0)
                def _():
                    coefs_z.wait_recv()
                    for off in range(1, NX):
                        coef_x(NX - off, at(s, off, 0)).start()

                arrived(GAX, xa.at[t, 0, pl.ds(1, NX - 1)])
                for k in (3, 4, 5, 1, 2, 6, 7):
                    j = slot_from(ORDER[k])
                    send(SENT_GAZ, GAZ + chunk_of(j), xa.at[t, 0], xa.at[t, j], at(s, 0, ORDER[k]))

        @pl.when(t == 0)
        def _():
            for load in loads[4:]:
                load.wait()
            for i in range(3):
                spare_copy(0, i, first_here).wait_recv()
            coefs_x.wait_recv()

        @pl.when(t == 1)
        def _():
            for i in range(3):
                spare_copy(1, i, first_here).wait_recv()

        gate_w, up_w, down_w = flat(gw.at[layer]), flat(uw.at[layer]), flat(dw.at[layer])
        contract = (((1,), (1,)), ((), ()))
        base = t * 16

        for c, (low, high) in enumerate(CHUNKS):
            blocks = pl.ds(low, high - low)
            rows = (high - low) * NX * tok
            span = pl.ds(low * NX * tok, rows)
            others = range(max(low, 1), high)
            lanes = lax.broadcasted_iota(jnp.int32, (rows, LANES), 1)
            unit = lax.broadcasted_iota(jnp.int32, (rows, units), 1)

            def product(ref, columns):
                values = flat(ref.at[t, blocks])[...]
                return tuple(
                    lax.dot_general(
                        values, weight[:, columns], contract, preferred_element_type=F32
                    )
                    for weight in (gate_w, up_w)
                )

            def part_a():
                arrived(GAZ + c, xa.at[t, pl.ds(others[0], len(others))])
                return product(xa, slice(0, aw))

            def part_b():
                for i in range(low, high):
                    gathered_x(i)
                return product(xb, slice(aw, width))

            if c == 0:
                (gate_b, up_b), (gate_a, up_a) = part_b(), part_a()
            else:
                (gate_a, up_a), (gate_b, up_b) = part_a(), part_b()
            gate, up = gate_a + gate_b, up_a + up_b
            factors = flat(coef.at[blocks])[...].astype(F32)

            def factor(which):
                spot = (lanes == base + which) | (lanes == base + which + 8)
                return jnp.sum(jnp.where(spot, factors, 0.0), axis=1, keepdims=True)

            scales = jnp.where(unit < home * tok, factor(x), factor(EXPERTS))
            hidden = gate / (1.0 + jnp.exp(-gate)) * up * scales
            hid[span] = hidden.astype(BF16)


            done = hid[span]

            def down(part, columns):
                value = jnp.dot(done, down_w[:, columns], preferred_element_type=F32)
                put(part.at[blocks], value.astype(BF16))

            down(pb, slice(lw, width))
            for i in sorted(range(low, high), key=BACK.index):
                for off in range(1, NX):
                    send(SENT_SX, SX + i, pb.at[i, off], rx.at[t, i, NX - off - 1], at(s, off, 0))
            down(pa, slice(0, lw))
            for i in others:
                j = slot_from(ORDER[i])
                send(SENT_SAZ, SAZ, pa.at[i], ra.at[t, j], at(s, 0, ORDER[i]))

        last = t == TICKS - 1
        to = jnp.where(last, s, s_after)
        for i in BACK:
            arrived(SX + i, rx.at[t, i])
            total = pb[i, 0].astype(F32)
            for o in range(1, NX):
                total = total + rx[t, i, o - 1].astype(F32)
            sb[t, i] = total.astype(BF16)
            if i > 0:
                back_b(t, i, at(to, 0, ORDER[i])).start()
            if i == A_AFTER:
                arrived(SAZ, ra.at[t, pl.ds(1, NZ - 1)])
                total = pa[0].astype(F32)
                for j in range(1, NZ):
                    total = total + ra[t, j].astype(F32)
                sa[t] = total.astype(BF16)
                for off in range(1, NX):
                    back_a(t, off, at(to, off, 0)).start()

        @pl.when(t < TICKS - 1)
        def _():
            for copy in back_own(t):
                copy.start()

        @pl.when(last)
        def _():
            parts_b[t, 0] = sb[t, 0]
            parts_a[t, 0] = sa[t, 0]

        left(SENT_GZ, xb.at[t, pl.ds(1, NZ - 1), 0])
        left(SENT_GX, xb.at[t, :, pl.ds(1, NX - 1)])
        left(SENT_GAX, xa.at[t, 0, pl.ds(1, NX - 1)])
        left(SENT_GAZ, xa.at[t, pl.ds(1, NZ - 1)])
        left(SENT_SX, rx.at[t])
        left(SENT_SAZ, ra.at[t, pl.ds(1, NZ - 1)])

        return carry

    lax.fori_loop(0, TICKS, tick, 0)
    out[:, :lw], out[:, lw:] = next_state(cur[TICKS - 1], TICKS - 1)
    for t in range(TICKS):
        for copies in back_groups(t):
            copies.wait_send()
        if t < TICKS - 1:
            for copy in back_own(t):
                copy.wait_send()
            res_copy(t).wait_send()
    for i in range(3):
        for order in range(2):
            spare_copy(order, i, first_there).wait_send()
    coefs_z.wait_send()
    coefs_x.wait_send()


def on_device(
    state, routes, gates, norm_gain, w_gate, w_up, w_down, spare_gate, spare_up, spare_down
):
    tok, width = state.shape[1:]
    home, extra = w_gate.shape[2], spare_gate.shape[2]
    units = -(-(home + extra) // 256) * 256
    aw = min(X_FIRST, width // 2)
    bw = width - aw
    lw = min(X_LAST, width // 2)
    rw = width - lw

    def cut(weights):
        return weights.reshape(2, weights.shape[2] // tok, tok, width)

    vmem, hbm = pl.BlockSpec(memory_space=pltpu.VMEM), pl.BlockSpec(memory_space=pltpu.HBM)
    store = pltpu.VMEM((2, units // tok, tok, width), BF16)
    dma = pltpu.SemaphoreType.DMA
    final = pl.pallas_call(
        functools.partial(kernel, lax.axis_size("segment")),
        out_shape=jax.ShapeDtypeStruct((tok, width), BF16),
        in_specs=[hbm] * 10,
        out_specs=vmem,
        scratch_shapes=[
            pltpu.VMEM((TICKS, tok, width), BF16),
            pltpu.VMEM((TICKS, 2, tok), jnp.int32),
            pltpu.VMEM((TICKS, 2, tok), F32),
            pltpu.VMEM((2, 1, width), F32),
            pltpu.VMEM((NZ, NX, tok, LANES), BF16),
            store,
            store,
            store,
            pltpu.VMEM((TICKS, NZ, NX, tok, aw), BF16),
            pltpu.VMEM((TICKS, NZ, NX, tok, bw), BF16),
            pltpu.VMEM((NZ * NX * tok, units), BF16),
            pltpu.VMEM((NZ, NX, tok, lw), BF16),
            pltpu.VMEM((NZ, NX, tok, rw), BF16),
            pltpu.VMEM((TICKS, NZ, NX, tok, lw), BF16),
            pltpu.VMEM((TICKS, NZ, NX - 1, tok, rw), BF16),
            pltpu.VMEM((TICKS, NX, tok, lw), BF16),
            pltpu.VMEM((TICKS, NZ, tok, rw), BF16),
            pltpu.VMEM((TICKS - 1, tok, width), BF16),
            pltpu.VMEM((TICKS, NX, tok, lw), BF16),
            pltpu.VMEM((TICKS, NZ, tok, rw), BF16),
            dma((6,)),
            dma((GROUPS,)),
            dma((TICKS, 4)),
            dma((TICKS, 4)),
            dma((TICKS - 1,)),
            dma((TICKS - 1,)),
            dma((7,)),
            dma((2, 3)),
            dma((2, 3)),
            dma((2,)),
            dma((2,)),
        ],
        compiler_params=pltpu.CompilerParams(
            collective_id=0, has_side_effects=True, vmem_limit_bytes=60 * 1024 * 1024
        ),
    )(
        state[0],
        jnp.swapaxes(routes[:, 0], 1, 2),
        jnp.swapaxes(gates[:, 0], 1, 2),
        norm_gain,
        cut(w_gate),
        cut(w_up),
        cut(w_down),
        cut(spare_gate),
        cut(spare_up),
        cut(spare_down),
    )
    return final[None]


def solution(mesh):
    return jax.shard_map(
        on_device,
        mesh=mesh,
        in_specs=(
            P("segment", "expert", None),
            P(None, "segment", "expert", None),
            P(None, "segment", "expert", None),
            P(None, "segment", None),
            P(None, "segment", "expert", None),
            P(None, "segment", "expert", None),
            P(None, "segment", "expert", None),
            P(None, "segment", "expert", None),
            P(None, "segment", "expert", None),
            P(None, "segment", "expert", None),
        ),
        out_specs=P("segment", "expert", None),
        check_vma=False,
    )
```

```python
import functools
import math

import jax
import jax.numpy as jnp
from jax import lax
from jax.experimental import pallas as pl
from jax.experimental.pallas import tpu as pltpu
from jax.sharding import PartitionSpec as P

EXPERTS = 4
TICKS = 4
CAP = 4
EPSILON = 1e-06
LANES = 128
MESH = pl.DeviceIdType.MESH
F32 = jnp.float32
BF16 = jnp.bfloat16

def group_of(section, tick_idx, segments):
    start = lax.rem(section - tick_idx + segments, segments)
    odd = lax.rem(start, 2) == 1
    first = jnp.where(odd & (start + TICKS <= segments), 1, 0)
    return first + jnp.where(start + tick_idx >= segments, 1, 0)


ORDER = (0, 1, -1, 4, 3, -3, 2, -2)
NZ, NX = 8, 4
X_FIRST = 512
X_LAST = 512
GX, SX, GZ, GAX, SAZ, GAZ = 0, 8, 16, 24, 25, 26
CHUNKS = ((0, 4), (4, 6), (6, 8))
GROUPS = GAZ + len(CHUNKS)
SENT_GZ, SENT_GX, SENT_GAX, SENT_GAZ, SENT_SX, SENT_SAZ = range(6)
BACK = (1, 2, 3, 4, 5, 6, 7, 0)
A_AFTER = 5


def slot_from(offset):
    return next(i for i, d in enumerate(ORDER) if (d + offset) % NZ == 0)


def chunk_of(slot):
    return next(c for c, (low, high) in enumerate(CHUNKS) if low <= slot < high)


def flat(ref):
    return ref.reshape(math.prod(ref.shape[:-1]), ref.shape[-1])


def put(ref, value):
    flat(ref)[...] = value


def kernel(
    segments,
    state, routes, gates, gain, w_gate, w_up, w_down, spare_g, spare_u, spare_d,
    out,
    cur, routes_v, gates_v, gain_v, coef, gw, uw, dw, xa, xb, hid, pa, pb, ra, rx, sa, sb, res,
    parts_a, parts_b,
    send_sem, recv_sem, back_send, back_recv, res_send, res_recv, w_sem, spare_send, spare_recv, coef_send, coef_recv,
):
    tok, width = state.shape
    home, extra = w_gate.shape[1], spare_g.shape[1]
    units = gw.shape[1] * tok
    aw, lw = xa.shape[-1], pa.shape[-1]
    s = lax.axis_index("segment")
    mine = lax.axis_index("expert")
    x, z = mine // NZ, lax.rem(mine, NZ)
    s_after = lax.rem(s + 1, segments)
    s_before = lax.rem(s + segments - 1, segments)

    def at(section, off_x, off_z):
        return (section, lax.rem(x + off_x + NX, NX) * NZ + lax.rem(z + off_z + NZ, NZ))

    before, after = (s_before, mine), (s_after, mine)

    loads = []
    for i, (source, store) in enumerate(
        (
            (state, cur.at[0]),
            (routes, routes_v),
            (gates, gates_v),
            (gain, gain_v),
            (w_gate, gw.at[:, pl.ds(0, home)]),
            (w_up, uw.at[:, pl.ds(0, home)]),
            (w_down, dw.at[:, pl.ds(0, home)]),
        )
    ):
        load = pltpu.make_async_copy(source, store, w_sem.at[i])
        load.start()
        loads.append(load)

    barrier = pltpu.get_barrier_semaphore()
    peers = [at(s, off, 0) for off in range(1, NX)]
    peers += [at(s, 0, off) for off in range(1, NZ)]
    for section in (s_after, s_before):
        peers += [at(section, 0, off) for off in range(NZ)]
        peers += [at(section, off, 0) for off in range(1, NX)]
    for peer in peers:
        pl.semaphore_signal(barrier, inc=1, device_id=peer, device_id_type=MESH)

    for store in (gw, uw, dw):
        unused = gw.shape[1] - home - extra
        store[:, home + extra :] = jnp.zeros((2, unused, tok, width), BF16)

    lane = lax.broadcasted_iota(jnp.int32, (tok, LANES), 1)
    row = lax.broadcasted_iota(jnp.int32, (tok, LANES), 0)
    diagonal = row[:, :tok] == lane[:, :tok]
    label = (lane % 8).astype(F32)
    low, of_tick = (lane // 8) % 2, lane // 16

    def upright(line):
        line = jnp.broadcast_to(line, (tok, tok))
        return jnp.sum(jnp.where(diagonal, line, 0.0), axis=1, keepdims=True)

    for load in loads[:4]:
        load.wait()
    packed = jnp.zeros((tok, LANES), F32)
    for t in range(TICKS):
        chosen, weights = routes_v[t].astype(F32), gates_v[t]
        hit0, hit1 = upright(chosen[0:1]) == label, upright(chosen[1:2]) == label
        member = jnp.where(hit0 | hit1, 1.0, 0.0)
        whole = jnp.where(hit0, upright(weights[0:1]), 0.0)
        whole = whole + jnp.where(hit1, upright(weights[1:2]), 0.0)
        position = jnp.zeros((tok, LANES), F32)
        for i in range(tok - 1):
            position = position + jnp.where(row > i, member[i : i + 1], 0.0)
        inside = position < CAP
        over = jnp.where(inside | (lane >= EXPERTS), 0.0, whole)
        spill = jnp.sum(over, axis=1, keepdims=True)
        value = jnp.where(label == EXPERTS, spill, jnp.where(inside, whole, 0.0))
        top = value.astype(BF16).astype(F32)
        packed = jnp.where(of_tick == t, jnp.where(low == 1, value - top, top), packed)
    coef[0, 0] = packed.astype(BF16)

    pl.semaphore_wait(barrier, len(peers))

    def remote(source, target, sent, got, peer):
        return pltpu.make_async_remote_copy(
            source, target, sent, got, device_id=peer, device_id_type=MESH
        )

    first_there = group_of(s_before, 0, segments)
    first_here = group_of(s, 0, segments)
    spare_pairs = ((spare_g, gw), (spare_u, uw), (spare_d, dw))

    def spare_copy(order, i, first):
        source, store = spare_pairs[i]
        part = first if order == 0 else 1 - first
        return remote(
            source.at[part],
            store.at[part, pl.ds(home, extra)],
            spare_send.at[order, i],
            spare_recv.at[order, i],
            before,
        )

    def coef_z(j, peer):
        return remote(coef.at[0, 0], coef.at[j, 0], coef_send.at[0], coef_recv.at[0], peer)

    def coef_x(o, peer):
        return remote(coef.at[:, 0], coef.at[:, o], coef_send.at[1], coef_recv.at[1], peer)

    def group(ref, sent, got):
        return remote(ref, ref, sent, got, after)

    coefs_z = group(coef.at[pl.ds(1, NZ - 1), 0], coef_send.at[0], coef_recv.at[0])
    coefs_x = group(coef.at[:, pl.ds(1, NX - 1)], coef_send.at[1], coef_recv.at[1])

    def res_copy(t):
        return remote(cur.at[t], res.at[t], res_send.at[t], res_recv.at[t], after)

    def back_sem(t, i, first):
        n = first if i > 0 else first + 2
        return back_send.at[t, n], back_recv.at[t, n]

    def back_b(t, i, peer):
        return remote(sb.at[t, i], parts_b.at[t, slot_from(ORDER[i])], *back_sem(t, i, 0), peer)

    def back_a(t, off, peer):
        o = (NX - off) % NX
        return remote(sa.at[t, off], parts_a.at[t, o], *back_sem(t, off, 1), peer)

    def back_groups(t):
        return (
            group(parts_b.at[t, pl.ds(1, NZ - 1)], *back_sem(t, 1, 0)),
            group(parts_a.at[t, pl.ds(1, NX - 1)], *back_sem(t, 1, 1)),
        )

    def back_own(t):
        return back_b(t, 0, after), back_a(t, 0, after)

    def landed(t):
        for copies in back_groups(t):
            copies.wait_recv()

        @pl.when(t < TICKS - 1)
        def _():
            for copy in back_own(t):
                copy.wait_recv()

        sums = []
        for parts, count in ((parts_a, NX), (parts_b, NZ)):
            total = parts[t, 0].astype(F32)
            for j in range(1, count):
                total = total + parts[t, j].astype(F32)
            sums.append(total)
        return sums

    def next_state(base, t):
        sum_a, sum_b = landed(t)
        base = base.astype(F32)
        return (base[:, :lw] + sum_a).astype(BF16), (base[:, lw:] + sum_b).astype(BF16)

    def tick(t, carry):
        layer = group_of(s, t, segments)

        def send(sent, got, source, target, peer):
            remote(source, target, send_sem.at[sent], recv_sem.at[got], peer).start()

        def arrived(got, landing):
            group(landing, send_sem.at[0], recv_sem.at[got]).wait_recv()

        def left(sent, shape_of):
            group(shape_of, send_sem.at[sent], recv_sem.at[0]).wait_send()

        @pl.when(t > 0)
        def _():
            res_copy(t - 1).wait_recv()
            cur[t, :, :lw], cur[t, :, lw:] = next_state(res[t - 1], t - 1)

        values = cur[t].astype(F32)
        scale = lax.rsqrt(jnp.mean(values * values, axis=-1, keepdims=True) + EPSILON)
        normed = (values * scale * gain_v[layer]).astype(BF16)
        xa[t, 0, 0] = normed[:, :aw]
        xb[t, 0, 0] = normed[:, aw:]

        def gather_z(i):
            j = slot_from(ORDER[i])
            send(SENT_GZ, GZ + j, xb.at[t, 0, 0], xb.at[t, j, 0], at(s, 0, ORDER[i]))

        def gather_x(i):
            for off in range(1, NX):
                o = NX - off
                send(SENT_GX, GX + i, xb.at[t, i, 0], xb.at[t, i, o], at(s, off, 0))

        def gathered_x(i):
            arrived(GX + i, xb.at[t, i, pl.ds(1, NX - 1)])

        @pl.when(t == 0)
        def _():
            for i in range(1, NZ):
                coef_z(slot_from(ORDER[i]), at(s, 0, ORDER[i])).start()

        for off in range(1, NX):
            o = NX - off
            send(SENT_GAX, GAX, xa.at[t, 0, 0], xa.at[t, 0, o], at(s, off, 0))
        gather_z(1)
        gather_z(2)
        gather_x(0)
        for i in range(3, NZ):
            gather_z(i)

        @pl.when(t == 0)
        def _():
            for order in range(2):
                for i in range(3):
                    spare_copy(order, i, first_there).start()

        @pl.when(t < TICKS - 1)
        def _():
            res_copy(t).start()

        for i in range(1, NZ):
            arrived(GZ + i, xb.at[t, i, 0])
            gather_x(i)
            if i == 2:
                @pl.when(t == 0)
                def _():
                    coefs_z.wait_recv()
                    for off in range(1, NX):
                        coef_x(NX - off, at(s, off, 0)).start()

                arrived(GAX, xa.at[t, 0, pl.ds(1, NX - 1)])
                for k in (3, 4, 5, 1, 2, 6, 7):
                    j = slot_from(ORDER[k])
                    send(SENT_GAZ, GAZ + chunk_of(j), xa.at[t, 0], xa.at[t, j], at(s, 0, ORDER[k]))

        @pl.when(t == 0)
        def _():
            for load in loads[4:]:
                load.wait()
            for i in range(3):
                spare_copy(0, i, first_here).wait_recv()
            coefs_x.wait_recv()

        @pl.when(t == 1)
        def _():
            for i in range(3):
                spare_copy(1, i, first_here).wait_recv()

        gate_w, up_w, down_w = flat(gw.at[layer]), flat(uw.at[layer]), flat(dw.at[layer])
        contract = (((1,), (1,)), ((), ()))
        base = t * 16

        for c, (low, high) in enumerate(CHUNKS):
            blocks = pl.ds(low, high - low)
            rows = (high - low) * NX * tok
            span = pl.ds(low * NX * tok, rows)
            others = range(max(low, 1), high)
            lanes = lax.broadcasted_iota(jnp.int32, (rows, LANES), 1)
            unit = lax.broadcasted_iota(jnp.int32, (rows, units), 1)

            def product(ref, columns):
                values = flat(ref.at[t, blocks])[...]
                return tuple(
                    lax.dot_general(
                        values, weight[:, columns], contract, preferred_element_type=F32
                    )
                    for weight in (gate_w, up_w)
                )

            def part_a():
                arrived(GAZ + c, xa.at[t, pl.ds(others[0], len(others))])
                return product(xa, slice(0, aw))

            def part_b():
                for i in range(low, high):
                    gathered_x(i)
                return product(xb, slice(aw, width))

            if c == 0:
                (gate_b, up_b), (gate_a, up_a) = part_b(), part_a()
            else:
                (gate_a, up_a), (gate_b, up_b) = part_a(), part_b()
            gate, up = gate_a + gate_b, up_a + up_b
            factors = flat(coef.at[blocks])[...].astype(F32)

            def factor(which):
                spot = (lanes == base + which) | (lanes == base + which + 8)
                return jnp.sum(jnp.where(spot, factors, 0.0), axis=1, keepdims=True)

            scales = jnp.where(unit < home * tok, factor(x), factor(EXPERTS))
            hidden = gate / (1.0 + jnp.exp(-gate)) * up * scales
            hid[span] = hidden.astype(BF16)


            done = hid[span]

            def down(part, columns):
                value = jnp.dot(done, down_w[:, columns], preferred_element_type=F32)
                put(part.at[blocks], value.astype(BF16))

            down(pb, slice(lw, width))
            for i in (*others, 0) if high == NZ else others:
                for off in range(1, NX):
                    send(SENT_SX, SX + i, pb.at[i, off], rx.at[t, i, NX - off - 1], at(s, off, 0))
            down(pa, slice(0, lw))
            for i in others:
                j = slot_from(ORDER[i])
                send(SENT_SAZ, SAZ, pa.at[i], ra.at[t, j], at(s, 0, ORDER[i]))

        last = t == TICKS - 1
        to = jnp.where(last, s, s_after)
        for i in BACK:
            arrived(SX + i, rx.at[t, i])
            total = pb[i, 0].astype(F32)
            for o in range(1, NX):
                total = total + rx[t, i, o - 1].astype(F32)
            sb[t, i] = total.astype(BF16)
            if i > 0:
                back_b(t, i, at(to, 0, ORDER[i])).start()
            if i == A_AFTER:
                arrived(SAZ, ra.at[t, pl.ds(1, NZ - 1)])
                total = pa[0].astype(F32)
                for j in range(1, NZ):
                    total = total + ra[t, j].astype(F32)
                sa[t] = total.astype(BF16)
                for off in range(1, NX):
                    back_a(t, off, at(to, off, 0)).start()

        @pl.when(t < TICKS - 1)
        def _():
            for copy in back_own(t):
                copy.start()

        @pl.when(last)
        def _():
            parts_b[t, 0] = sb[t, 0]
            parts_a[t, 0] = sa[t, 0]

        left(SENT_GZ, xb.at[t, pl.ds(1, NZ - 1), 0])
        left(SENT_GX, xb.at[t, :, pl.ds(1, NX - 1)])
        left(SENT_GAX, xa.at[t, 0, pl.ds(1, NX - 1)])
        left(SENT_GAZ, xa.at[t, pl.ds(1, NZ - 1)])
        left(SENT_SX, rx.at[t])
        left(SENT_SAZ, ra.at[t, pl.ds(1, NZ - 1)])

        return carry

    lax.fori_loop(0, TICKS, tick, 0)
    out[:, :lw], out[:, lw:] = next_state(cur[TICKS - 1], TICKS - 1)
    for t in range(TICKS):
        for copies in back_groups(t):
            copies.wait_send()
        if t < TICKS - 1:
            for copy in back_own(t):
                copy.wait_send()
            res_copy(t).wait_send()
    for i in range(3):
        for order in range(2):
            spare_copy(order, i, first_there).wait_send()
    coefs_z.wait_send()
    coefs_x.wait_send()


def on_device(
    state, routes, gates, norm_gain, w_gate, w_up, w_down, spare_gate, spare_up, spare_down
):
    tok, width = state.shape[1:]
    home, extra = w_gate.shape[2], spare_gate.shape[2]
    units = -(-(home + extra) // 256) * 256
    aw = min(X_FIRST, width // 2)
    bw = width - aw
    lw = min(X_LAST, width // 2)
    rw = width - lw

    def cut(weights):
        return weights.reshape(2, weights.shape[2] // tok, tok, width)

    vmem, hbm = pl.BlockSpec(memory_space=pltpu.VMEM), pl.BlockSpec(memory_space=pltpu.HBM)
    store = pltpu.VMEM((2, units // tok, tok, width), BF16)
    dma = pltpu.SemaphoreType.DMA
    final = pl.pallas_call(
        functools.partial(kernel, lax.axis_size("segment")),
        out_shape=jax.ShapeDtypeStruct((tok, width), BF16),
        in_specs=[hbm] * 10,
        out_specs=vmem,
        scratch_shapes=[
            pltpu.VMEM((TICKS, tok, width), BF16),
            pltpu.VMEM((TICKS, 2, tok), jnp.int32),
            pltpu.VMEM((TICKS, 2, tok), F32),
            pltpu.VMEM((2, 1, width), F32),
            pltpu.VMEM((NZ, NX, tok, LANES), BF16),
            store,
            store,
            store,
            pltpu.VMEM((TICKS, NZ, NX, tok, aw), BF16),
            pltpu.VMEM((TICKS, NZ, NX, tok, bw), BF16),
            pltpu.VMEM((NZ * NX * tok, units), BF16),
            pltpu.VMEM((NZ, NX, tok, lw), BF16),
            pltpu.VMEM((NZ, NX, tok, rw), BF16),
            pltpu.VMEM((TICKS, NZ, NX, tok, lw), BF16),
            pltpu.VMEM((TICKS, NZ, NX - 1, tok, rw), BF16),
            pltpu.VMEM((TICKS, NX, tok, lw), BF16),
            pltpu.VMEM((TICKS, NZ, tok, rw), BF16),
            pltpu.VMEM((TICKS - 1, tok, width), BF16),
            pltpu.VMEM((TICKS, NX, tok, lw), BF16),
            pltpu.VMEM((TICKS, NZ, tok, rw), BF16),
            dma((6,)),
            dma((GROUPS,)),
            dma((TICKS, 4)),
            dma((TICKS, 4)),
            dma((TICKS - 1,)),
            dma((TICKS - 1,)),
            dma((7,)),
            dma((2, 3)),
            dma((2, 3)),
            dma((2,)),
            dma((2,)),
        ],
        compiler_params=pltpu.CompilerParams(
            collective_id=0, has_side_effects=True, vmem_limit_bytes=60 * 1024 * 1024
        ),
    )(
        state[0],
        jnp.swapaxes(routes[:, 0], 1, 2),
        jnp.swapaxes(gates[:, 0], 1, 2),
        norm_gain,
        cut(w_gate),
        cut(w_up),
        cut(w_down),
        cut(spare_gate),
        cut(spare_up),
        cut(spare_down),
    )
    return final[None]


def solution(mesh):
    return jax.shard_map(
        on_device,
        mesh=mesh,
        in_specs=(
            P("segment", "expert", None),
            P(None, "segment", "expert", None),
            P(None, "segment", "expert", None),
            P(None, "segment", None),
            P(None, "segment", "expert", None),
            P(None, "segment", "expert", None),
            P(None, "segment", "expert", None),
            P(None, "segment", "expert", None),
            P(None, "segment", "expert", None),
            P(None, "segment", "expert", None),
        ),
        out_specs=P("segment", "expert", None),
        check_vma=False,
    )
```
